128 devices in a mesh: face: 8 (over z, x_lo), tile: 16 (over y, x_hi, core).
Axes of the slice: x: 4 (x_hi: 2, x_lo: 2; x = x_hi * 2 + x_lo), y: 4, z: 4, core: 2. Of those that a mesh axis runs over, the one named last changes fastest.
Arguments:
- atmosphere: float32 [192, 64, 4096], P(None, 'face', 'tile'), may hold values from -6 to 6
- ocean: float32 [96, 256, 2048], P(None, 'tile', 'face'), may hold values from -6 to 6
- kernel_atm: float32 [192, 49], replicated, may hold values from -0.875 to 0.875
- w_in_atm: float32 [192, 768], replicated, may hold values from -0.4375 to 0.4375
- w_out_atm: float32 [192, 768], replicated, may hold values from -0.21875 to 0.21875
- w_flux: float32 [64, 192], replicated, may hold values from -0.4375 to 0.4375
- kernel_ocean: float32 [96, 49], replicated, may hold values from -0.875 to 0.875
- w_in_ocean: float32 [96, 384], replicated, may hold values from -0.625 to 0.625
- w_out_ocean: float32 [96, 384], replicated, may hold values from -0.3125 to 0.3125
- w_couple: float32 [96, 64], replicated, may hold values from -0.75 to 0.75
- intersection_src: int32 [8, 512, 4], P('face', 'tile'), may hold values from 0 to 255, as said below
- intersection_count: int32 [8, 512], P('face', 'tile'), may hold values from 1 to 4
- intersection_weight: float32 [8, 512, 4, 128, 128], P('face', 'tile'), may hold values from -0.25 to 0.25
Outputs:
- atm_next: float32 [192, 64, 4096], P(None, 'face', 'tile')
- ocean_next: float32 [96, 256, 2048], P(None, 'tile', 'face')
The draws below stay inside these ranges and needn't reach their ends.
Inputs may be any that keep to these rules, and one draw needn't show every extreme that they name: `intersection_src`: entries at slots k >= intersection_count are padding and name some block. Among the live pairs of the 32 ocean blocks of one device, at most 8 name blocks of one atmosphere tile, and in every device some tile is named by exactly 8 of them.
All inputs are finite; a program needn't handle non-finite values.
Results may differ from the reference program's by a relative error of at most 0.0003.
Values sent between devices are 32-bit elements; how exact they have to be, the bound alone decides.
A program may use at most 128 MiB of HBM per device.

```python
import jax
import jax.numpy as jnp
from jax import lax

CA = 192
HA = 768
CO = 96
HO = 384
FL = 64
BLK = 128
K = 4
AXD = 8
AYD = 256
OYD = 16
OXD = 256
NAX = 64
NAY = 4096
NOLAT = 256
NOLON = 2048
BA = 16
BO = 32
N_FACE = 8
N_TILE = 16


def draw_intersection_src(key, part):
    key = jax.random.fold_in(key, 11)
    key_shift, key_inner = jax.random.split(key)
    blocks = jnp.arange(N_TILE * BO, dtype=jnp.int32)
    dst_tile = blocks // BO
    group_index = blocks % BO // (BO // N_TILE)
    offsets = jax.random.randint(key_shift, (N_FACE, N_TILE), 0, N_TILE, dtype=jnp.int32)
    source_tile = (dst_tile[None, :] + offsets[:, dst_tile] + group_index[None, :]) % N_TILE
    within = jax.random.randint(key_inner, (N_FACE, N_TILE * BO, K), 0, BA, dtype=jnp.int32)
    return (source_tile[:, :, None] * BA + within).astype(jnp.int32)


def draw_intersection_count(key, part):
    key = jax.random.fold_in(key, 23)
    key_group, key_count = jax.random.split(key)
    group_index = jnp.arange(N_TILE * BO, dtype=jnp.int32) % BO // (BO // N_TILE)
    full_group = jax.random.randint(key_group, (N_FACE, N_TILE), 0, N_TILE, dtype=jnp.int32)
    full_each = jnp.repeat(full_group, BO, axis=1)
    counts = jax.random.randint(key_count, (N_FACE, N_TILE * BO), 1, K + 1, dtype=jnp.int32)
    return jnp.where(group_index[None, :] == full_each, K, counts).astype(jnp.int32)


def block_scale(stream_key, extent, pieces, least, largest):
    level, own = 1.0, jax.random.fold_in(stream_key, 6)
    for dim, shards_of in pieces:
        steps = jnp.exp(jax.random.uniform(jax.random.fold_in(own, dim), (shards_of,), jnp.float32, least / len(pieces), largest / len(pieces)))
        level = level * jnp.repeat(steps, extent[dim] // shards_of).reshape([-1 if axis == dim else 1 for axis in range(len(extent))])
    return level


def normal_values(rng, extent, width, reach, cuts=(), kind=jnp.bfloat16):
    result = jax.random.normal(rng, extent, jnp.float32) * width
    if len(cuts) > 0:
        result = block_scale(rng, extent, cuts, -0.22, 0.18) * result
    return jnp.clip(result, min=-reach, max=reach).astype(kind)


def setup_inputs(seed: int = 0) -> dict:
    key_of = jax.random.split(jax.random.key(seed), 14)
    return {
        "atmosphere": normal_values(key_of[0], (CA, NAX, NAY), 1.0, 6.0, ((1, 8), (2, 16)), jnp.float32),
        "ocean": normal_values(key_of[1], (CO, NOLAT, NOLON), 1.0, 6.0, ((1, 16), (2, 8)), jnp.float32),
        "kernel_atm": normal_values(key_of[2], (CA, 49), 49 ** -0.5, 0.875, (), jnp.float32),
        "w_in_atm": normal_values(key_of[3], (CA, HA), CA ** -0.5, 0.4375, (), jnp.float32),
        "w_out_atm": normal_values(key_of[4], (CA, HA), HA ** -0.5, 0.21875, (), jnp.float32),
        "w_flux": normal_values(key_of[5], (FL, CA), CA ** -0.5, 0.4375, (), jnp.float32),
        "kernel_ocean": normal_values(key_of[6], (CO, 49), 49 ** -0.5, 0.875, (), jnp.float32),
        "w_in_ocean": normal_values(key_of[7], (CO, HO), CO ** -0.5, 0.625, (), jnp.float32),
        "w_out_ocean": normal_values(key_of[8], (CO, HO), HO ** -0.5, 0.3125, (), jnp.float32),
        "w_couple": normal_values(key_of[9], (CO, FL), FL ** -0.5, 0.75, (), jnp.float32),
        "intersection_src": draw_intersection_src(jax.random.fold_in(key_of[13], 71), 0),
        "intersection_count": draw_intersection_count(jax.random.fold_in(key_of[13], 71), 0),
        "intersection_weight": normal_values(key_of[12], (N_FACE, N_TILE * BO, K, BLK, BLK), (K * BLK) ** -0.5, 0.25, ((0, 8), (1, 16)), jnp.float32),
    }


HIGHEST = lax.Precision.HIGHEST

def depthwise(padded, kernel, row_count, col_count):
    running = jnp.zeros((padded.shape[0], row_count, col_count), jnp.float32)
    for shift_row in range(7):
        for shift_col in range(7):
            weight_here = kernel[:, shift_row * 7 + shift_col][:, None, None]
            running = running + weight_here * padded[:, shift_row:shift_row + row_count, shift_col:shift_col + col_count]
    return running

def normalize(values):
    average = lax.optimization_barrier(jnp.mean(values, axis=0, keepdims=True))
    centred = values - average
    spread = lax.optimization_barrier(jnp.mean(centred * centred, axis=0, keepdims=True))
    return centred * lax.rsqrt(spread + 1e-06)

def mixer(normed, w_in, w_out):
    hidden = jax.nn.gelu(jnp.einsum('ch,cxy->hxy', w_in, normed, precision=HIGHEST), approximate=False)
    return jnp.einsum('ch,hxy->cxy', w_out, hidden, precision=HIGHEST)

def reference(atmosphere, ocean, kernel_atm, w_in_atm, w_out_atm, w_flux, kernel_ocean, w_in_ocean, w_out_ocean, w_couple, intersection_src, intersection_count, intersection_weight):
    padded = jnp.pad(atmosphere, ((0, 0), (3, 3), (3, 3)), mode='wrap')

    def atm_slab(face_index):
        start_row = (face_index * AXD).astype(jnp.int32)
        slab_rows = lax.dynamic_slice_in_dim(padded, start_row, AXD + 6, 1)
        filtered = depthwise(slab_rows, kernel_atm, AXD, AYD * N_TILE)
        centre = lax.dynamic_slice_in_dim(atmosphere, start_row, AXD, 1)
        stepped = centre + mixer(normalize(filtered), w_in_atm, w_out_atm)
        latent = jnp.einsum('fc,cxy->fxy', w_flux, stepped, precision=HIGHEST)
        return (stepped, latent)
    slabs, latents = lax.map(atm_slab, jnp.arange(N_FACE, dtype=jnp.int32))
    atm_next = slabs.transpose(1, 0, 2, 3).reshape(CA, NAX, NAY)
    face_blocks = latents.reshape(N_FACE, FL, AXD, N_TILE, AYD // BLK, BLK)
    face_blocks = face_blocks.transpose(0, 3, 2, 4, 1, 5).reshape(N_FACE, N_TILE * BA, FL, BLK)
    active = jnp.arange(K, dtype=jnp.int32)[None, None, :] < intersection_count[:, :, None]

    def regrid(face_index):
        face_flux = face_blocks[face_index]
        selected = face_flux[intersection_src[face_index]]
        selected = jnp.where(active[face_index][:, :, None, None], selected, 0.0)
        return jnp.einsum('pkfi,pkio->pfo', selected, intersection_weight[face_index], precision=HIGHEST)
    regridded = lax.map(regrid, jnp.arange(N_FACE, dtype=jnp.int32))
    flux_grid = regridded.reshape(N_FACE, N_TILE, OYD, OXD // BLK, FL, BLK)
    flux_grid = flux_grid.transpose(4, 1, 2, 0, 3, 5).reshape(FL, NOLAT, NOLON)
    lon_pad = jnp.pad(ocean, ((0, 0), (0, 0), (3, 3)), mode='wrap')
    southern = jnp.zeros((CO, 3, NOLON + 6), jnp.float32)
    northern = lon_pad[:, NOLAT - 3:, :][:, ::-1, ::-1]
    ocean_pad = jnp.concatenate([southern, lon_pad, northern], axis=1)
    filtered_sea = depthwise(ocean_pad, kernel_ocean, NOLAT, NOLON)
    mixed_in = normalize(filtered_sea) + jnp.einsum('cf,fxy->cxy', w_couple, flux_grid, precision=HIGHEST)

    def band_mix(band_index):
        band_rows = lax.dynamic_slice_in_dim(mixed_in, (band_index * OYD).astype(jnp.int32), OYD, 1)
        return mixer(band_rows, w_in_ocean, w_out_ocean)
    bands = lax.map(band_mix, jnp.arange(N_TILE, dtype=jnp.int32))
    ocean_next = ocean + bands.transpose(1, 0, 2, 3).reshape(CO, NOLAT, NOLON)
    return (atm_next, ocean_next)
```

```python
import functools

import jax
import jax.numpy as jnp
from jax import lax
from jax.experimental import pallas as pl
from jax.experimental.pallas import tpu as pltpu
from jax.sharding import PartitionSpec as P

F32 = jnp.float32
BF16 = jnp.bfloat16
MESH = pl.DeviceIdType.MESH
MIB = 2**20
VMEM = pl.BlockSpec(memory_space=pltpu.VMEM)
SMEM = pl.BlockSpec(memory_space=pltpu.SMEM)
ANY = pl.BlockSpec(memory_space=pl.ANY)
DMA = pltpu.SemaphoreType.DMA

CA, HA, CO, HO, FL = 192, 768, 96, 384, 64
AR, OR, COLS = 8, 16, 256
N_FACE, N_TILE = 8, 16


def split(x):
    hi = x.astype(BF16)
    return hi, (x - hi.astype(F32)).astype(BF16)


def mm(a, b):
    return jnp.dot(a, b, preferred_element_type=F32)


def mm3(a, b):
    return mm(a[0], b[0]) + (mm(a[1], b[0]) + mm(a[0], b[1]))


def gelu(x):
    return 0.5 * x * (1.0 + lax.erf(x * 0.7071067811865476))


def layer_norm(v):
    centred = v - jnp.mean(v, axis=0, keepdims=True)
    spread = jnp.mean(centred * centred, axis=0, keepdims=True)
    return centred * lax.rsqrt(spread + 1e-06)


def lanes():
    return lax.broadcasted_iota(jnp.int32, (8, 128), 1)


def group(g):
    return pl.ds(pl.multiple_of(g * 8, 8), 8)


def rows_out_of(raw, rows, channels, wide):
    for half in range(2):
        flat = raw.at[half].reshape(channels * rows, 128)
        for r in range(rows):
            wide[r, :, half * 128 : half * 128 + 128] = flat[pl.ds(r, channels, stride=rows), :]


def pack_edges(wide, first, rows, right, left):
    span = 4 * rows
    slots = 128 // span

    def step(v, carry):
        lane = lanes()
        to_right = jnp.zeros((8, 128), F32)
        to_left = jnp.zeros((8, 128), F32)
        for s in range(slots):
            here = group(v * slots + s)
            for r in range(rows):
                at = s * span + 4 * r
                mask = (lane >= at) & (lane < at + 3)
                last = wide[first + r, here, 128:256]
                initial = wide[first + r, here, 0:128]
                to_right = jnp.where(mask, pltpu.roll(last, (at - 125) % 128, 1), to_right)
                to_left = jnp.where(mask, pltpu.roll(initial, at, 1) if at else initial, to_left)
        right[group(v), :] = to_right
        left[group(v), :] = to_left
        return carry

    lax.fori_loop(0, 6, step, 0)


def unpack_edges(pairs, rows, halo):
    span = 4 * rows
    slots = 128 // span

    def step(v, carry):
        lane = lanes()
        for s in range(slots):
            here = group(v * slots + s)
            for target, source, from_left, from_right in pairs:
                at = s * span + 4 * source
                after = from_right[group(v), :]
                before = from_left[group(v), :]
                after = pltpu.roll(after, (128 - at) % 128, 1) if at else after
                before = pltpu.roll(before, (125 - at) % 128, 1)
                halo[target, here, :] = jnp.where(lane < 3, after, jnp.where(lane >= 125, before, 0.0))
        return carry

    lax.fori_loop(0, 6, step, 0)


def spread_taps(kernel_ref, channels, table):
    kernel = jnp.transpose(kernel_ref[...])
    for tap in range(49):
        table[tap] = jnp.broadcast_to(kernel[:, tap : tap + 1], (channels, 128))


def depthwise(wide, halo, table, channels, tops, base, out):
    needed = sorted({t + i for t in tops for i in range(7)})

    def step(g, carry):
        here = group(g)
        lane = lanes()
        sums = [[jnp.zeros((8, 128), F32)] * 2 for _ in tops]
        for j in range(7):
            shift = j - 3
            weights = [table[i * 7 + j, here, :] for i in range(7)]
            for row in needed:
                a = wide[base + row, here, 0:128]
                b = wide[base + row, here, 128:256]
                if shift > 0:
                    keep = lane < 128 - shift
                    c = pltpu.roll(halo[base + row, here, :], 128 - shift, 1)
                    a = pltpu.roll(a, 128 - shift, 1)
                    b = pltpu.roll(b, 128 - shift, 1)
                    a, b = jnp.where(keep, a, b), jnp.where(keep, b, c)
                elif shift < 0:
                    keep = lane >= -shift
                    c = pltpu.roll(halo[base + row, here, :], -shift, 1)
                    a = pltpu.roll(a, -shift, 1)
                    b = pltpu.roll(b, -shift, 1)
                    a, b = jnp.where(keep, a, c), jnp.where(keep, b, a)
                for n, t in enumerate(tops):
                    i = row - t
                    if 0 <= i < 7:
                        sums[n] = [sums[n][0] + weights[i] * a, sums[n][1] + weights[i] * b]
        for n in range(len(tops)):
            out[n, here, 0:128] = sums[n][0]
            out[n, here, 128:256] = sums[n][1]
        return carry

    lax.fori_loop(0, channels // 8, step, 0)


def mixer(normed, w_in, w_out, hidden, chunk=256):
    size = w_in[0].shape[0]
    for start in range(0, size, chunk):
        part = pl.ds(start, min(chunk, size - start))
        value = gelu(mm3((w_in[0][part, :], w_in[1][part, :]), normed))
        hidden[0][part, :], hidden[1][part, :] = split(value)
    return mm3((w_out[0][...], w_out[1][...]), (hidden[0][...], hidden[1][...]))


def position():
    face = lax.axis_index("face")
    tile = lax.axis_index("tile")
    return face, tile


def ring(value, step, count):
    return lax.rem(value + (step + count), count)


def halo_kernel(
    atm_hbm, sea_hbm, aw, ah, sw, sh,
    atm_raw, sea_raw, a_out, a_in, s_out, s_in, mirror_w, mirror_h,
    load_sem, send_sem, recv_sem,
):
    face, tile = position()
    up, down = ring(face, 1, N_FACE), ring(face, -1, N_FACE)
    north, south = ring(tile, 1, N_TILE), ring(tile, -1, N_TILE)
    loads = []
    for half in range(2):
        cut = pl.ds(128 * half, 128)
        loads.append(pltpu.make_async_copy(atm_hbm.at[:, :, cut], atm_raw.at[half], load_sem.at[half]))
        loads.append(pltpu.make_async_copy(sea_hbm.at[:, :, cut], sea_raw.at[half], load_sem.at[2 + half]))
    for load in loads:
        load.start()
    barrier = pltpu.get_barrier_semaphore()
    near = [
        (up, tile), (down, tile), (face, north), (face, south),
        (up, north), (up, south), (down, north), (down, south),
    ]
    for device in near:
        pl.semaphore_signal(barrier, inc=1, device_id=device, device_id_type=MESH)
    top = tile == N_TILE - 1
    across = (N_FACE - 1 - face, tile)

    @pl.when(top)
    def _():
        pl.semaphore_signal(barrier, inc=1, device_id=across, device_id_type=MESH)

    pl.semaphore_wait(barrier, len(near) + tile // (N_TILE - 1))

    def copy(k, src, dst, device):
        return pltpu.make_async_remote_copy(
            src_ref=src, dst_ref=dst, send_sem=send_sem.at[k], recv_sem=recv_sem.at[k],
            device_id=device, device_id_type=MESH,
        )

    loads[0].wait()
    loads[2].wait()
    rows_out_of(atm_raw, AR, CA, aw.at[pl.ds(3, AR)])
    copies = []
    for d in range(3):
        copies.append(copy(2 * d, aw.at[10 - d], aw.at[2 - d], (up, tile)))
        copies.append(copy(2 * d + 1, aw.at[3 + d], aw.at[11 + d], (down, tile)))
    for c in copies:
        c.start()
    pack_edges(aw, 3, AR, a_out.at[0], a_out.at[1])
    for n, f in enumerate((up, face, down)):
        copies.append(copy(6 + n, a_out.at[0], a_in.at[0, n], (f, north)))
        copies.append(copy(9 + n, a_out.at[1], a_in.at[1, n], (f, south)))
    for c in copies[6:]:
        c.start()
    loads[1].wait()
    loads[3].wait()
    rows_out_of(sea_raw, OR, CO, sw.at[pl.ds(3, OR)])
    first = len(copies)
    copies.append(copy(12, sw.at[pl.ds(16, 3)], sw.at[pl.ds(0, 3)], (face, north)))
    copies.append(copy(13, sw.at[pl.ds(3, 3)], sw.at[pl.ds(19, 3)], (face, south)))
    for c in copies[first:]:
        c.start()
    pack_edges(sw, 3, OR, s_out.at[0], s_out.at[1])
    first = len(copies)
    for n, t in enumerate((north, tile, south)):
        copies.append(copy(14 + n, s_out.at[0], s_in.at[0, n], (up, t)))
        copies.append(copy(17 + n, s_out.at[1], s_in.at[1, n], (down, t)))
    for c in copies[first:]:
        c.start()
    for c in copies[6:12]:
        c.wait()
    rows = [(r, AR - 3 + r, a_in.at[0, 0], a_in.at[1, 0]) for r in range(3)]
    rows += [(3 + r, r, a_in.at[0, 1], a_in.at[1, 1]) for r in range(AR)]
    rows += [(3 + AR + r, r, a_in.at[0, 2], a_in.at[1, 2]) for r in range(3)]
    unpack_edges(rows, AR, ah)
    for c in copies[12:]:
        c.wait()
    rows = [(r, OR - 3 + r, s_in.at[0, 0], s_in.at[1, 0]) for r in range(3)]
    rows += [(3 + r, r, s_in.at[0, 1], s_in.at[1, 1]) for r in range(OR)]
    rows += [(3 + OR + r, r, s_in.at[0, 2], s_in.at[1, 2]) for r in range(3)]
    unpack_edges(rows, OR, sh)

    @pl.when(tile == 0)
    def _():
        sw[0:3] = jnp.zeros((3, CO, COLS), F32)
        sh[0:3] = jnp.zeros((3, CO, 128), F32)

    @pl.when(top)
    def _():
        fold = [
            copy(20, sw.at[pl.ds(16, 3)], mirror_w, across),
            copy(21, sh.at[pl.ds(16, 3)], mirror_h, across),
        ]
        for c in fold:
            c.start()
        for c in fold:
            c.wait()
        flip = 127 - lax.broadcasted_iota(jnp.int32, (CO, 128), 1)
        for k in range(3):
            sw[19 + k, :, 0:128] = jnp.take_along_axis(mirror_w[2 - k, :, 128:256], flip, axis=1)
            sw[19 + k, :, 128:256] = jnp.take_along_axis(mirror_w[2 - k, :, 0:128], flip, axis=1)
            sh[19 + k] = jnp.take_along_axis(mirror_h[2 - k], flip, axis=1)

    for c in copies[:6]:
        c.wait()


def exchange(atmosphere, ocean):
    return pl.pallas_call(
        halo_kernel,
        out_shape=(
            jax.ShapeDtypeStruct((AR + 6, CA, COLS), F32),
            jax.ShapeDtypeStruct((AR + 6, CA, 128), F32),
            jax.ShapeDtypeStruct((OR + 6, CO, COLS), F32),
            jax.ShapeDtypeStruct((OR + 6, CO, 128), F32),
        ),
        in_specs=[ANY, ANY],
        out_specs=(VMEM,) * 4,
        scratch_shapes=[
            pltpu.VMEM((2, CA, AR, 128), F32),
            pltpu.VMEM((2, CO, OR, 128), F32),
            pltpu.VMEM((2, 48, 128), F32),
            pltpu.VMEM((2, 3, 48, 128), F32),
            pltpu.VMEM((2, 48, 128), F32),
            pltpu.VMEM((2, 3, 48, 128), F32),
            pltpu.VMEM((3, CO, COLS), F32),
            pltpu.VMEM((3, CO, 128), F32),
            DMA((4,)),
            DMA((22,)),
            DMA((22,)),
        ],
        compiler_params=pltpu.CompilerParams(
            collective_id=0, has_side_effects=True, vmem_limit_bytes=50 * MIB
        ),
        name="halo",
    )(atmosphere, ocean)


def place(row):
    return (3 - row) * 4 if row < 4 else (row - 4) * 4 + 2


def atm_kernel(
    aw, ah, kernel_ref, w_in_ref, w_out_ref, w_flux_ref, out, lat,
    table, conv, wi, wo, wf, normed, hidden, back,
):
    spread_taps(kernel_ref, CA, table)
    wi[0], wi[1] = split(jnp.transpose(w_in_ref[...]))
    wo[0], wo[1] = split(w_out_ref[...])
    wf[0], wf[1] = split(w_flux_ref[...])
    for stage in range(4):
        tops = (3 - stage, 4 + stage)
        depthwise(aw, ah, table, CA, tops, 0, conv)
        for n in range(2):
            cut = slice(n * COLS, n * COLS + COLS)
            normed[0, :, cut], normed[1, :, cut] = split(layer_norm(conv[n]))
        mixed = mixer(
            (normed[0], normed[1]), (wi.at[0], wi.at[1]), (wo.at[0], wo.at[1]),
            (hidden.at[0], hidden.at[1]),
        )
        for n, row in enumerate(tops):
            value = aw[3 + row] + mixed[:, n * COLS : n * COLS + COLS]
            flux = mm3((wf[0], wf[1]), split(value))
            for half in range(2):
                cut = slice(half * 128, half * 128 + 128)
                lat[place(row) + half] = flux[:, cut]
                back.at[half].reshape(CA * AR, 128)[pl.ds(row, CA, stride=AR), :] = value[:, cut]
    for half in range(2):
        out[:, :, half * 128 : half * 128 + 128] = back[half]


def atm_step(aw, ah, kernel_atm, w_in, w_out, w_flux):
    return pl.pallas_call(
        atm_kernel,
        out_shape=(
            jax.ShapeDtypeStruct((CA, AR, COLS), F32),
            jax.ShapeDtypeStruct((16, FL, 128), F32),
        ),
        in_specs=[VMEM] * 6,
        out_specs=(VMEM,) * 2,
        scratch_shapes=[
            pltpu.VMEM((49, CA, 128), F32),
            pltpu.VMEM((2, CA, COLS), F32),
            pltpu.VMEM((2, HA, CA), BF16),
            pltpu.VMEM((2, CA, HA), BF16),
            pltpu.VMEM((2, FL, CA), BF16),
            pltpu.VMEM((2, CA, 2 * COLS), BF16),
            pltpu.VMEM((2, HA, 2 * COLS), BF16),
            pltpu.VMEM((2, CA, AR, 128), F32),
        ],
        compiler_params=pltpu.CompilerParams(vmem_limit_bytes=50 * MIB),
        name="atmosphere",
    )(aw, ah, kernel_atm, w_in, w_out, w_flux)


def gather_kernel(lat, out, send_sem, recv_sem):
    face, tile = position()
    y, x, core = tile // 4, lax.rem(tile // 2, 2), lax.rem(tile, 2)

    def at(dy, dx, dc):
        return (ring(y, dy, 4) * 2 + lax.rem(x + dx, 2)) * 2 + lax.rem(core + dc, 2)

    targets = [at(0, 1, 0), at(1, 0, 0), at(-1, 0, 0), at(2, 0, 0), at(0, 0, 1)]
    barrier = pltpu.get_barrier_semaphore()
    for target in targets:
        pl.semaphore_signal(barrier, inc=1, device_id=(face, target), device_id_type=MESH)
    pl.semaphore_wait(barrier, len(targets))
    out[tile] = lat[...]

    def copy(stage, kind, block, target):
        part = out.at[block, pl.ds(4 * stage, 4)]
        return pltpu.make_async_remote_copy(
            src_ref=part, dst_ref=part, send_sem=send_sem.at[stage, kind], recv_sem=recv_sem.at[stage, kind],
            device_id=(face, target), device_id_type=MESH,
        )

    partner = at(0, 1, 0)
    steps = ((1, 1), (2, -1), (3, 2))
    sends = []
    for stage in range(4):
        mine = [copy(stage, 0, tile, partner)]
        mine += [copy(stage, kind, tile, at(dy, 0, 0)) for kind, dy in steps]
        mine += [copy(stage, 7, tile, at(0, 0, 1))]
        for c in mine:
            c.start()
        sends += mine
    for stage in range(4):
        copy(stage, 0, partner, partner).wait_recv()
        mine = [copy(stage, kind + 3, partner, at(dy, 0, 0)) for kind, dy in steps]
        mine += [copy(stage, 8, partner, at(0, 0, 1))]
        for c in mine:
            c.start()
        sends += mine
    for stage in range(4):
        for hop in range(2):
            for kind, dy in steps:
                block = at(-dy, hop, 0)
                copy(stage, kind + 3 * hop, block, partner).wait_recv()
                c = copy(stage, 8 + kind + 3 * hop, block, at(0, 0, 1))
                c.start()
                sends.append(c)
    for stage in range(4):
        copy(stage, 7, at(0, 0, 1), partner).wait_recv()
        copy(stage, 8, at(0, 1, 1), partner).wait_recv()
        for hop in range(2):
            for kind, dy in steps:
                copy(stage, 8 + kind + 3 * hop, at(-dy, hop, 1), partner).wait_recv()
    for c in sends:
        c.wait_send()


def gather(lat):
    return pl.pallas_call(
        gather_kernel,
        out_shape=jax.ShapeDtypeStruct((N_TILE, 16, FL, 128), F32),
        in_specs=[VMEM],
        out_specs=VMEM,
        scratch_shapes=[DMA((4, 15)), DMA((4, 15))],
        compiler_params=pltpu.CompilerParams(
            collective_id=1, has_side_effects=True, vmem_limit_bytes=50 * MIB
        ),
        name="gather",
    )(lat)


def ocean_kernel(
    src, count, sw, sh, blocks, weights, kernel_ref, w_in_ref, w_out_ref, w_couple_ref, out,
    table, conv, wi, wo, wc, normed, hidden, back,
):
    step = pl.program_id(0)

    @pl.when(step == 0)
    def _():
        spread_taps(kernel_ref, CO, table)
        wi[0], wi[1] = split(jnp.transpose(w_in_ref[...]))
        wo[0], wo[1] = split(w_out_ref[...])
        wc[0], wc[1] = split(jnp.transpose(w_couple_ref[...]))

    base = 2 * step
    depthwise(sw, sh, table, CO, (0, 1), base, conv)
    for n in range(2):
        for half in range(2):
            local = 2 * n + half
            block = 4 * step + local
            live = count[block]
            picked = []
            for k in range(4):
                index = src[k, block]
                t, a = index // 16, lax.rem(index, 16)
                r = a // 2
                spot = jnp.where(r < 4, (3 - r) * 4, (r - 4) * 4 + 2) + lax.rem(a, 2)
                picked.append(jnp.where(k < live, blocks[t, spot], 0.0))
            left = split(jnp.concatenate(picked, axis=1))
            right = split(weights[local].reshape(512, 128))
            flux = mm3(left, right)
            cut = slice(n * COLS + half * 128, n * COLS + half * 128 + 128)
            coupled = mm3((wc[0], wc[1]), split(flux))
            value = layer_norm(conv[n, :, half * 128 : half * 128 + 128]) + coupled
            normed[0, :, cut], normed[1, :, cut] = split(value)
    mixed = mixer(
        (normed[0], normed[1]), (wi.at[0], wi.at[1]), (wo.at[0], wo.at[1]),
        (hidden.at[0], hidden.at[1]), 128,
    )
    for n in range(2):
        value = sw[base + 3 + n] + mixed[:, n * COLS : n * COLS + COLS]
        for half in range(2):
            flat = back.at[half].reshape(CO * OR, 128)
            flat[pl.ds(base + n, CO, stride=OR), :] = value[:, half * 128 : half * 128 + 128]

    @pl.when(step == OR // 2 - 1)
    def _():
        for half in range(2):
            out[:, :, half * 128 : half * 128 + 128] = back[half]


def ocean_step(src, count, sw, sh, blocks, weights, kernel_ocean, w_in, w_out, w_couple):
    whole = lambda *shape: pl.BlockSpec(shape, lambda i: (0,) * len(shape))
    return pl.pallas_call(
        ocean_kernel,
        grid=(OR // 2,),
        out_shape=jax.ShapeDtypeStruct((CO, OR, COLS), F32),
        in_specs=[
            SMEM, SMEM,
            whole(OR + 6, CO, COLS), whole(OR + 6, CO, 128), whole(N_TILE, 16, FL, 128),
            pl.BlockSpec((4, 4, 128, 128), lambda i: (i, 0, 0, 0)),
            whole(49, CO), whole(CO, HO), whole(CO, HO), whole(FL, CO),
        ],
        out_specs=whole(CO, OR, COLS),
        scratch_shapes=[
            pltpu.VMEM((49, CO, 128), F32),
            pltpu.VMEM((2, CO, COLS), F32),
            pltpu.VMEM((2, HO, CO), BF16),
            pltpu.VMEM((2, CO, HO), BF16),
            pltpu.VMEM((2, CO, FL), BF16),
            pltpu.VMEM((2, CO, 2 * COLS), BF16),
            pltpu.VMEM((2, HO, 2 * COLS), BF16),
            pltpu.VMEM((2, CO, OR, 128), F32),
        ],
        compiler_params=pltpu.CompilerParams(vmem_limit_bytes=56 * MIB),
        name="ocean",
    )(src, count, sw, sh, blocks, weights, kernel_ocean, w_in, w_out, w_couple)


def body(
    atmosphere, ocean, kernel_atm, w_in_atm, w_out_atm, w_flux, kernel_ocean, w_in_ocean,
    w_out_ocean, w_couple, intersection_src, intersection_count, intersection_weight,
):
    aw, ah, sw, sh = exchange(atmosphere, ocean)
    atm_next, lat = atm_step(aw, ah, kernel_atm.T, w_in_atm, w_out_atm, w_flux)
    blocks = gather(lat)
    ocean_next = ocean_step(
        intersection_src[0].T, intersection_count[0], sw, sh, blocks, intersection_weight[0],
        kernel_ocean.T, w_in_ocean, w_out_ocean, w_couple.T,
    )
    return (atm_next, ocean_next)


def solution(mesh):
    return jax.shard_map(
        body,
        mesh=mesh,
        in_specs=(
            P(None, "face", "tile"),
            P(None, "tile", "face"),
            P(), P(), P(), P(), P(), P(), P(), P(),
            P("face", "tile", None),
            P("face", "tile"),
            P("face", "tile", None, None, None),
        ),
        out_specs=(P(None, "face", "tile"), P(None, "tile", "face")),
        check_vma=False,
    )
```

```python
import jax
import jax.numpy as jnp
from jax import lax
from jax.experimental import pallas as pl
from jax.experimental.pallas import tpu as pltpu
from jax.sharding import PartitionSpec as P

F32 = jnp.float32
BF16 = jnp.bfloat16
MESH = pl.DeviceIdType.MESH
MIB = 2**20
VMEM = pl.BlockSpec(memory_space=pltpu.VMEM)
SMEM = pl.BlockSpec(memory_space=pltpu.SMEM)
ANY = pl.BlockSpec(memory_space=pl.ANY)
DMA = pltpu.SemaphoreType.DMA

CA, HA, CO, HO, FL = 192, 768, 96, 384, 64
AR, OR, COLS = 8, 16, 256
N_FACE, N_TILE = 8, 16
EDGE = 8
STAGES = ((3, 4), (2, 5), (1, 6), (0, 7))
PIECES = ((3, 4, 5, 6, 7), (8, 9, 10, 11, 12), (0, 1, 2), (13, 14, 15))


def split(x):
    hi = x.astype(BF16)
    return hi, (x - hi.astype(F32)).astype(BF16)


def mm(a, b):
    return jnp.dot(a, b, preferred_element_type=F32)


def mm_t(a, b):
    return lax.dot_general(a, b, (((1,), (1,)), ((), ())), preferred_element_type=F32)


def gelu(x):
    return 0.5 * x * (1.0 + lax.erf(x * 0.7071067811865476))


def lane_sum(x, ones):
    hi, rest = x.astype(BF16), x
    rest = rest - hi.astype(F32)
    mid, low = split(rest)
    return mm(hi, ones) + (mm(mid, ones) + mm(low, ones))


def one_where(condition):
    return jnp.where(condition, 1.0, 0.0).astype(BF16)


def swap_halves(x):
    return pltpu.roll(x, 64, 1)


def rows_out_of(raw, rows, channels, wide):
    for half in range(2):
        flat = raw.at[half].reshape(channels * rows, 128)
        for r in range(rows):
            wide[r, :, half * 128 : half * 128 + 128] = flat[pl.ds(r, channels, stride=rows), :]


def turn_atm(wide, turned_a, turned_b, row):
    for half in range(2):
        cut = slice(half * 128, half * 128 + 128)
        turned_a[row, EDGE + half * 128 : EDGE + half * 128 + 128, :] = jnp.transpose(wide[row, 0:128, cut])
    both = jnp.concatenate([wide[row, 128:CA, 0:128], wide[row, 128:CA, 128:256]], axis=0)
    turned_b[row, EDGE : EDGE + 128, :] = jnp.transpose(both)


def turn_sea(values, turned, row):
    for half in range(2):
        cut = slice(half * 128, half * 128 + 128)
        full = jnp.concatenate([values[:, cut], jnp.zeros((128 - CO, 128), F32)], axis=0)
        turned[row, EDGE + half * 128 : EDGE + half * 128 + 128, :] = jnp.transpose(full)


def depthwise(src, taps, tops, cols, out, m):
    needed = sorted({t + i for t in tops for i in range(7)})

    def step(g, carry):
        start = g * (8 * m)
        sums = [[jnp.zeros((8, 128), F32) for _ in range(m)] for _ in tops]
        for j in range(7):
            weights = [taps[i * 7 + j] for i in range(7)]
            for row in needed:
                for b in range(m):
                    v = src[row, pl.ds(start + (8 * b + EDGE - 3 + j), 8), :]
                    for n, t in enumerate(tops):
                        if 0 <= row - t < 7:
                            sums[n][b] = sums[n][b] + weights[row - t] * v
        for n in range(len(tops)):
            for b in range(m):
                out[n, pl.ds(pl.multiple_of(start + 8 * b, 8), 8), :] = sums[n][b]
        return carry

    lax.fori_loop(0, cols // (8 * m), step, 0)


def ring(value, step, count):
    return lax.rem(value + (step + count), count)


def fused_kernel(
    src, count, atm_hbm, sea_hbm, weights_hbm,
    kernel_atm, w_in_atm, w_out_atm, w_flux, kernel_sea, w_in_sea, w_out_sea, w_couple,
    atm_out, sea_out,
    atm_raw, sea_raw, aw, ata, atb, sw, st,
    a_out, a_in, s_out, s_in, mirror_w, mirror_out, mirror_in,
    taps_a, taps_b, taps_s, conv_a, conv_b, conv_s,
    wi_a, wo_a, wf_a, hidden, wi_s, wo_s, wic_s, pre, blocks, slots, w_hi, w_lo, back_a, back_s,
    load_sem, slot_sem, out_sem, send_sem, recv_sem, flux_send, flux_recv,
):
    face, tile = lax.axis_index("face"), lax.axis_index("tile")
    up, down = ring(face, 1, N_FACE), ring(face, -1, N_FACE)
    north, south = ring(tile, 1, N_TILE), ring(tile, -1, N_TILE)
    y, x, core = tile // 4, lax.rem(tile // 2, 2), lax.rem(tile, 2)
    top = tile == N_TILE - 1
    across = (N_FACE - 1 - face, tile)

    def at(dy, dx, dc):
        return (ring(y, dy, 4) * 2 + lax.rem(x + dx, 2)) * 2 + lax.rem(core + dc, 2)

    partner, sibling = at(0, 1, 0), at(0, 0, 1)

    loads = []
    for half in range(2):
        cut = pl.ds(128 * half, 128)
        loads.append(pltpu.make_async_copy(atm_hbm.at[:, :, cut], atm_raw.at[half], load_sem.at[half]))
    for half in range(2):
        cut = pl.ds(128 * half, 128)
        loads.append(pltpu.make_async_copy(sea_hbm.at[:, :, cut], sea_raw.at[half], load_sem.at[2 + half]))
    for load in loads:
        load.start()

    def weight_load(n):
        return pltpu.make_async_copy(weights_hbm.at[pl.ds(4 * n, 4)], slots.at[n % 2], slot_sem.at[n % 2])

    weight_load(0).start()
    weight_load(1).start()

    barrier = pltpu.get_barrier_semaphore()
    near = [
        (up, tile), (down, tile), (face, north), (face, south),
        (up, north), (up, south), (down, north), (down, south),
        (face, partner), (face, at(1, 0, 0)), (face, at(-1, 0, 0)), (face, at(2, 0, 0)),
    ]
    for device in near:
        pl.semaphore_signal(barrier, inc=1, device_id=device, device_id_type=MESH)

    @pl.when(top)
    def _():
        pl.semaphore_signal(barrier, inc=1, device_id=across, device_id_type=MESH)

    def copy(k, src_ref, dst_ref, device):
        return pltpu.make_async_remote_copy(
            src_ref=src_ref, dst_ref=dst_ref, send_sem=send_sem.at[k], recv_sem=recv_sem.at[k],
            device_id=device, device_id_type=MESH,
        )

    loads[0].wait()
    loads[1].wait()
    rows_out_of(atm_raw, AR, CA, aw.at[pl.ds(3, AR)])
    pl.semaphore_wait(barrier, len(near) + tile // (N_TILE - 1))
    row_copies = []
    for d in range(3):
        row_copies.append(copy(2 * d, aw.at[10 - d], aw.at[2 - d], (up, tile)))
        row_copies.append(copy(2 * d + 1, aw.at[3 + d], aw.at[11 + d], (down, tile)))
    for c in row_copies:
        c.start()

    for r in range(AR):
        turn_atm(aw, ata, atb, 3 + r)
    for r in range(AR):
        to = pl.ds(4 * r, 3)
        a_out[0, to, :] = ata[3 + r, pl.ds(EDGE + COLS - 3, 3), :]
        a_out[1, to, :] = ata[3 + r, pl.ds(EDGE, 3), :]
        to = pl.ds(32 + 4 * r, 3)
        a_out[0, to, :] = swap_halves(atb[3 + r, pl.ds(EDGE + 125, 3), :])
        a_out[1, to, :] = swap_halves(atb[3 + r, pl.ds(EDGE, 3), :])
    edge_copies = []
    for n, f in enumerate((up, face, down)):
        edge_copies.append(copy(6 + n, a_out.at[0], a_in.at[0, n], (f, north)))
        edge_copies.append(copy(9 + n, a_out.at[1], a_in.at[1, n], (f, south)))
    for n in (2, 3, 0, 1, 4, 5):
        edge_copies[n].start()

    def atm_edges(row):
        n = 0 if row < 3 else 1 if row < 3 + AR else 2
        r = (row - 3) % AR
        low = lax.broadcasted_iota(jnp.int32, (3, 128), 1) < 64
        frm = pl.ds(4 * r, 3)
        ata[row, pl.ds(EDGE - 3, 3), :] = a_in[0, n, frm, :]
        ata[row, pl.ds(EDGE + COLS, 3), :] = a_in[1, n, frm, :]
        frm = pl.ds(32 + 4 * r, 3)
        inner = swap_halves(atb[row, pl.ds(EDGE + 125, 3), :])
        outer = swap_halves(atb[row, pl.ds(EDGE, 3), :])
        atb[row, pl.ds(EDGE - 3, 3), :] = jnp.where(low, a_in[0, n, frm, :], inner)
        atb[row, pl.ds(EDGE + 128, 3), :] = jnp.where(low, outer, a_in[1, n, frm, :])

    for t in range(49):
        k = kernel_atm[t : t + 1, :]
        taps_a[t] = jnp.broadcast_to(k[:, 0:128], (8, 128))
        taps_b[t] = jnp.broadcast_to(jnp.concatenate([k[:, 128:CA], k[:, 128:CA]], axis=1), (8, 128))
    turned = jnp.transpose(w_in_atm[...])
    gap = jnp.zeros((HA, 64), F32)
    for n, full in enumerate(
        (jnp.concatenate([turned, gap], axis=1), jnp.concatenate([turned[:, 0:128], gap, turned[:, 128:CA]], axis=1))
    ):
        hi, lo = split(full)
        for c in range(3):
            wi_a[n, c, 0:256, :] = hi[256 * c : 256 * c + 256]
            wi_a[n, c, 256:512, :] = lo[256 * c : 256 * c + 256]
    wo_a[0:CA, :], wo_a[CA : 2 * CA, :] = split(w_out_atm[...])
    wf_a[0:FL, :], wf_a[FL : 2 * FL, :] = split(w_flux[...])
    depth = lax.broadcasted_iota(jnp.int32, (256, 128), 0)
    lane = lax.broadcasted_iota(jnp.int32, (256, 128), 1)
    ones_first = one_where(depth < CA)
    ones_second = one_where((depth < 128) | (depth >= CA))

    def mm_stacked(stack, size, right):
        both = mm(stack, right[0])
        return both[0:size] + (both[size : 2 * size] + mm(stack[0:size], right[1]))

    def atm_stage(stage):
        tops = STAGES[stage]
        depthwise(ata, taps_a, tops, 256, conv_a, 4)
        depthwise(atb, taps_b, tops, 128, conv_b, 4)
        b = jnp.concatenate([conv_b[0], conv_b[1]], axis=0)
        a1 = jnp.concatenate([conv_a[0, 0:128], conv_a[1, 0:128]], axis=0)
        a2 = jnp.concatenate([conv_a[0, 128:256], conv_a[1, 128:256]], axis=0)
        m1 = lane_sum(jnp.concatenate([a1, b], axis=1), ones_first) * (1.0 / CA)
        m2 = lane_sum(jnp.concatenate([a2, b], axis=1), ones_second) * (1.0 / CA)
        a1, a2, b = a1 - m1, a2 - m2, b - jnp.where(lane < 64, m1, m2)
        v1 = lane_sum(jnp.concatenate([a1 * a1, b * b], axis=1), ones_first) * (1.0 / CA)
        v2 = lane_sum(jnp.concatenate([a2 * a2, b * b], axis=1), ones_second) * (1.0 / CA)
        r1, r2 = lax.rsqrt(v1 + 1e-06), lax.rsqrt(v2 + 1e-06)
        b = b * jnp.where(lane < 64, r1, r2)
        normed = (
            split(jnp.concatenate([a1 * r1, b], axis=1)),
            split(jnp.concatenate([a2 * r2, b], axis=1)),
        )
        for c in range(3):
            for half in range(2):
                hi, lo = normed[half]
                both = mm_t(wi_a[half, c], hi)
                value = gelu(both[0:256] + (both[256:512] + mm_t(wi_a[half, c, 0:256], lo)))
                to = (slice(256 * c, 256 * c + 256), slice(256 * half, 256 * half + 256))
                hidden[(0, *to)], hidden[(1, *to)] = split(value)
        for half in range(2):
            cut = slice(256 * half, 256 * half + 256)
            mixed = mm_stacked(wo_a[...], CA, (hidden[0, :, cut], hidden[1, :, cut]))
            here = slice(half * 128, half * 128 + 128)
            value = mixed + jnp.concatenate([aw[3 + row, :, here] for row in tops], axis=1)
            flux = mm_stacked(wf_a[...], FL, split(value))
            for n, row in enumerate(tops):
                part = slice(n * 128, n * 128 + 128)
                blocks[tile, 4 * stage + 2 * n + half] = flux[:, part]
                back_a.at[half].reshape(CA * AR, 128)[pl.ds(row, CA, stride=AR), :] = value[:, part]

    def flux_copy(stage, kind, block, target):
        part = blocks.at[block, pl.ds(4 * stage, 4)]
        return pltpu.make_async_remote_copy(
            src_ref=part, dst_ref=part, send_sem=flux_send.at[stage, kind], recv_sem=flux_recv.at[stage, kind],
            device_id=(face, target), device_id_type=MESH,
        )

    hops = ((1, 1), (2, -1), (3, 2))
    sent = []

    def start(mine):
        for c in mine:
            c.start()
        sent.extend(mine)

    def send_own(stage):
        start([flux_copy(stage, 0, tile, partner)])
        start([flux_copy(stage, kind, tile, at(dy, 0, 0)) for kind, dy in hops])
        start([flux_copy(stage, 7, tile, sibling)])

    def relay(stage):
        flux_copy(stage, 0, partner, partner).wait_recv()
        start([flux_copy(stage, kind + 3, partner, at(dy, 0, 0)) for kind, dy in hops])
        start([flux_copy(stage, 8, partner, sibling)])

    def forward(stage, hop):
        for kind, dy in hops:
            block = at(-dy, hop, 0)
            flux_copy(stage, kind + 3 * hop, block, partner).wait_recv()
            start([flux_copy(stage, 8 + kind + 3 * hop, block, sibling)])

    def finish(stage):
        flux_copy(stage, 7, sibling, partner).wait_recv()
        flux_copy(stage, 8, at(0, 1, 1), partner).wait_recv()
        for hop in range(2):
            for kind, dy in hops:
                flux_copy(stage, 8 + kind + 3 * hop, at(-dy, hop, 1), partner).wait_recv()

    for n in (2, 3):
        edge_copies[n].wait_recv()
    for r in range(AR):
        atm_edges(3 + r)
    atm_stage(0)
    send_own(0)

    loads[2].wait()
    loads[3].wait()
    rows_out_of(sea_raw, OR, CO, sw.at[pl.ds(3, OR)])
    sea_copies = [
        copy(12, sw.at[pl.ds(16, 3)], sw.at[pl.ds(0, 3)], (face, north)),
        copy(13, sw.at[pl.ds(3, 3)], sw.at[pl.ds(19, 3)], (face, south)),
    ]
    for r in range(OR):
        turn_sea(sw[3 + r], st, 3 + r)
    for r in range(OR):
        to = pl.ds(4 * r, 3)
        s_out[0, to, :] = st[3 + r, pl.ds(EDGE + COLS - 3, 3), :]
        s_out[1, to, :] = st[3 + r, pl.ds(EDGE, 3), :]
    for n, t in enumerate((north, tile, south)):
        sea_copies.append(copy(14 + n, s_out.at[0], s_in.at[0, n], (up, t)))
        sea_copies.append(copy(17 + n, s_out.at[1], s_in.at[1, n], (down, t)))
    for c in sea_copies[2:]:
        c.start()
    for t in range(49):
        k = jnp.concatenate([kernel_sea[t : t + 1, :], jnp.zeros((1, 128 - CO), F32)], axis=1)
        taps_s[t] = jnp.broadcast_to(k, (8, 128))
    turned = jnp.transpose(w_in_sea[...])
    hi, lo = split(jnp.concatenate([turned, jnp.zeros((HO, 128 - CO), F32)], axis=1))
    wi_s[:, 0:128] = hi
    wi_s[:, 128:256] = lo
    wo_s[0:CO, :], wo_s[CO : 2 * CO, :] = split(w_out_sea[...])
    left = split(turned)
    right = split(jnp.transpose(w_couple[...]))
    hi, lo = split(mm(left[0], right[0]) + (mm(left[1], right[0]) + mm(left[0], right[1])))
    wic_s[...] = jnp.concatenate([hi, hi, lo], axis=1)
    ones_sea = one_where(depth[0:128] < CO)

    def sea_edges(row, n, r):
        frm = pl.ds(4 * r, 3)
        st[row, pl.ds(EDGE - 3, 3), :] = s_in[0, n, frm, :]
        st[row, pl.ds(EDGE + COLS, 3), :] = s_in[1, n, frm, :]

    def sea_piece(piece):
        tops = PIECES[piece]
        depthwise(st, taps_s, tops, 256, conv_s, 2)
        for n, row in enumerate(tops):
            c = conv_s[n]
            c = c - lane_sum(c, ones_sea) * (1.0 / CO)
            spread = lane_sum(c * c, ones_sea) * (1.0 / CO)
            hi, lo = split(c * lax.rsqrt(spread + 1e-06))
            pre[row] = mm_t(wi_s[...], jnp.concatenate([hi, hi], axis=1)) + mm_t(wi_s[:, 0:128], lo)

    def split_weights(n):
        weight_load(n).wait()

        def step(b, carry):
            w_hi[4 * n + b], w_lo[4 * n + b] = split(slots[n % 2, b].reshape(512, 128))
            return carry

        lax.fori_loop(0, 4, step, 0)
        if n + 2 < 8:
            weight_load(n + 2).start()

    for n in (2, 3):
        sea_copies[2 + n].wait_recv()
    for r in range(OR):
        sea_edges(3 + r, 1, r)
    sea_piece(0)

    def atm_rows(d):
        row_copies[2 * d].wait_recv()
        row_copies[2 * d + 1].wait_recv()
        if d == 0:
            for n in (0, 1, 4, 5):
                edge_copies[n].wait_recv()
        for row in (2 - d, 11 + d):
            turn_atm(aw, ata, atb, row)
            atm_edges(row)

    atm_rows(0)
    atm_stage(1)
    send_own(1)
    relay(0)
    for c in sea_copies[:2]:
        c.start()

    fold = [
        copy(20, sw.at[pl.ds(16, 3)], mirror_w, across),
        copy(21, mirror_out, mirror_in, across),
    ]

    @pl.when(top)
    def _():
        for r in range(3):
            mirror_out[pl.ds(8 * r, 3), :] = st[16 + r, pl.ds(EDGE - 3, 3), :]
            mirror_out[pl.ds(8 * r + 4, 3), :] = st[16 + r, pl.ds(EDGE + COLS, 3), :]
        for c in fold:
            c.start()

    sea_piece(1)
    split_weights(0)
    split_weights(1)
    atm_rows(1)
    atm_stage(2)
    send_own(2)
    relay(1)
    forward(0, 0)
    split_weights(2)
    split_weights(3)
    atm_rows(2)
    atm_stage(3)
    send_own(3)
    relay(2)
    forward(0, 1)
    forward(1, 0)
    atm_store = []
    for half in range(2):
        cut = pl.ds(128 * half, 128)
        atm_store.append(pltpu.make_async_copy(back_a.at[half], atm_out.at[:, :, cut], out_sem.at[half]))
    for c in atm_store:
        c.start()
    for n in range(4, 8):
        split_weights(n)
    relay(3)
    forward(1, 1)
    forward(2, 0)

    for n in (0, 1, 4, 5):
        sea_copies[2 + n].wait_recv()
    for c in sea_copies[:2]:
        c.wait_recv()
    for r in range(3):
        turn_sea(sw[r], st, r)
        sea_edges(r, 0, OR - 3 + r)
        turn_sea(sw[3 + OR + r], st, 3 + OR + r)
        sea_edges(3 + OR + r, 2, r)

    @pl.when(tile == 0)
    def _():
        st[0:3] = jnp.zeros((3, COLS + 2 * EDGE, 128), F32)

    @pl.when(top)
    def _():
        for c in fold:
            c.wait()
        flip = 127 - lax.broadcasted_iota(jnp.int32, (CO, 128), 1)
        for k in range(3):
            first = jnp.take_along_axis(mirror_w[2 - k, :, 128:256], flip, axis=1)
            second = jnp.take_along_axis(mirror_w[2 - k, :, 0:128], flip, axis=1)
            turn_sea(jnp.concatenate([first, second], axis=1), st, 19 + k)
            for c in range(3):
                st[19 + k, pl.ds(EDGE - 3 + c, 1), :] = mirror_in[pl.ds(8 * (2 - k) + 4 + 2 - c, 1), :]
                st[19 + k, pl.ds(EDGE + COLS + c, 1), :] = mirror_in[pl.ds(8 * (2 - k) + 2 - c, 1), :]

    sea_piece(2)
    sea_piece(3)
    forward(2, 1)
    forward(3, 0)
    forward(3, 1)
    for stage in range(4):
        finish(stage)

    def sea_row(q):
        fluxes = []
        for half in range(2):
            block = 2 * q + half
            live = count[block]
            picked = []
            for k in range(4):
                index = src[k, block]
                t, a = index // 16, lax.rem(index, 16)
                r = a // 2
                spot = jnp.where(r < 4, (3 - r) * 4, (r - 4) * 4 + 2) + lax.rem(a, 2)
                picked.append(jnp.where(k < live, blocks[t, spot], 0.0))
            hi, lo = split(jnp.concatenate(picked, axis=1))
            both = mm(jnp.concatenate([hi, lo], axis=0), w_hi[block])
            fluxes.append(both[0:FL] + (both[FL : 2 * FL] + mm(hi, w_lo[block])))
        hi, lo = split(jnp.concatenate(fluxes, axis=1))
        grown = split(gelu(pre[q] + mm(wic_s[...], jnp.concatenate([hi, lo, hi], axis=0))))
        value = sw[3 + q] + mm_stacked(wo_s[...], CO, grown)
        for half in range(2):
            flat = back_s.at[half].reshape(CO * OR, 128)
            flat[pl.ds(q, CO, stride=OR), :] = value[:, half * 128 : half * 128 + 128]

    sea_store = []
    for part in range(2):

        def step(i, carry, part=part):
            sea_row(8 * part + 2 * i)
            sea_row(8 * part + 2 * i + 1)
            return carry

        lax.fori_loop(0, 4, step, 0)
        for half in range(2):
            rows, cut = pl.ds(8 * part, 8), pl.ds(128 * half, 128)
            c = pltpu.make_async_copy(
                back_s.at[half, :, rows], sea_out.at[:, rows, cut], out_sem.at[2 + 2 * part + half]
            )
            c.start()
            sea_store.append(c)
    for c in row_copies + edge_copies + sea_copies + sent:
        c.wait_send()
    for c in atm_store + sea_store:
        c.wait()


def step(src, count, atmosphere, ocean, weights, *params):
    return pl.pallas_call(
        fused_kernel,
        out_shape=(
            jax.ShapeDtypeStruct((CA, AR, COLS), F32),
            jax.ShapeDtypeStruct((CO, OR, COLS), F32),
        ),
        in_specs=[SMEM, SMEM, ANY, ANY, ANY] + [VMEM] * 8,
        out_specs=(ANY, ANY),
        scratch_shapes=[
            pltpu.VMEM((2, CA, AR, 128), F32),
            pltpu.VMEM((2, CO, OR, 128), F32),
            pltpu.VMEM((AR + 6, CA, COLS), F32),
            pltpu.VMEM((AR + 6, COLS + 2 * EDGE, 128), F32),
            pltpu.VMEM((AR + 6, 128 + 2 * EDGE, 128), F32),
            pltpu.VMEM((OR + 6, CO, COLS), F32),
            pltpu.VMEM((OR + 6, COLS + 2 * EDGE, 128), F32),
            pltpu.VMEM((2, 64, 128), F32),
            pltpu.VMEM((2, 3, 64, 128), F32),
            pltpu.VMEM((2, 64, 128), F32),
            pltpu.VMEM((2, 3, 64, 128), F32),
            pltpu.VMEM((3, CO, COLS), F32),
            pltpu.VMEM((24, 128), F32),
            pltpu.VMEM((24, 128), F32),
            pltpu.VMEM((49, 8, 128), F32),
            pltpu.VMEM((49, 8, 128), F32),
            pltpu.VMEM((49, 8, 128), F32),
            pltpu.VMEM((2, 256, 128), F32),
            pltpu.VMEM((2, 128, 128), F32),
            pltpu.VMEM((5, 256, 128), F32),
            pltpu.VMEM((2, 3, 512, 256), BF16),
            pltpu.VMEM((2 * CA, HA), BF16),
            pltpu.VMEM((2 * FL, CA), BF16),
            pltpu.VMEM((2, HA, 2 * COLS), BF16),
            pltpu.VMEM((HO, 256), BF16),
            pltpu.VMEM((2 * CO, HO), BF16),
            pltpu.VMEM((HO, 3 * FL), BF16),
            pltpu.VMEM((OR, HO, COLS), F32),
            pltpu.VMEM((N_TILE, 16, FL, 128), F32),
            pltpu.VMEM((2, 4, 4, 128, 128), F32),
            pltpu.VMEM((32, 512, 128), BF16),
            pltpu.VMEM((32, 512, 128), BF16),
            pltpu.VMEM((2, CA, AR, 128), F32),
            pltpu.VMEM((2, CO, OR, 128), F32),
            DMA((4,)),
            DMA((2,)),
            DMA((6,)),
            DMA((22,)),
            DMA((22,)),
            DMA((4, 15)),
            DMA((4, 15)),
        ],
        compiler_params=pltpu.CompilerParams(
            collective_id=0, has_side_effects=True, vmem_limit_bytes=58 * MIB
        ),
        name="coupled",
    )(src, count, atmosphere, ocean, weights, *params)


def body(
    atmosphere, ocean, kernel_atm, w_in_atm, w_out_atm, w_flux, kernel_ocean, w_in_ocean,
    w_out_ocean, w_couple, intersection_src, intersection_count, intersection_weight,
):
    return step(
        intersection_src[0].T, intersection_count[0], atmosphere, ocean, intersection_weight[0],
        kernel_atm.T, w_in_atm, w_out_atm, w_flux, kernel_ocean.T, w_in_ocean, w_out_ocean, w_couple.T,
    )


def solution(mesh):
    return jax.shard_map(
        body,
        mesh=mesh,
        in_specs=(
            P(None, "face", "tile"),
            P(None, "tile", "face"),
            P(), P(), P(), P(), P(), P(), P(), P(),
            P("face", "tile", None),
            P("face", "tile"),
            P("face", "tile", None, None, None),
        ),
        out_specs=(P(None, "face", "tile"), P(None, "tile", "face")),
        check_vma=False,
    )
```

```python
import jax
import jax.numpy as jnp
from jax import lax
from jax.experimental import pallas as pl
from jax.experimental.pallas import tpu as pltpu
from jax.sharding import PartitionSpec as P

F32 = jnp.float32
BF16 = jnp.bfloat16
MESH = pl.DeviceIdType.MESH
MIB = 2**20
VMEM = pl.BlockSpec(memory_space=pltpu.VMEM)
SMEM = pl.BlockSpec(memory_space=pltpu.SMEM)
ANY = pl.BlockSpec(memory_space=pl.ANY)
DMA = pltpu.SemaphoreType.DMA

CA, HA, CO, HO, FL = 192, 768, 96, 384, 64
AR, OR, COLS = 8, 16, 256
N_FACE, N_TILE = 8, 16
EDGE = 8
STAGES = ((3, 4), (2, 5), (1, 6), (0, 7))
PIECES = ((3, 8), (8, 13), (0, 3), (13, 16))


def split(x):
    hi = x.astype(BF16)
    return hi, (x - hi.astype(F32)).astype(BF16)


def mm(a, b):
    return jnp.dot(a, b, preferred_element_type=F32)


def mm_t(a, b):
    return lax.dot_general(a, b, (((1,), (1,)), ((), ())), preferred_element_type=F32)


def gelu(x):
    return 0.5 * x * (1.0 + lax.erf(x * 0.7071067811865476))


def lane_sum(x, ones, parts):
    total = 0.0
    for _ in range(parts):
        part = x.astype(BF16)
        x = x - part.astype(F32)
        total = total + mm(part, ones)
    return total


def one_where(condition):
    return jnp.where(condition, 1.0, 0.0).astype(BF16)


def swap_halves(x):
    return pltpu.roll(x, 64, 1)


def rows_out_of(raw, rows, channels, wide):
    for half in range(2):
        flat = raw.at[half].reshape(channels * rows, 128)
        for r in range(rows):
            wide[r, :, half * 128 : half * 128 + 128] = flat[pl.ds(r, channels, stride=rows), :]


def turn_atm(wide, turned_a, turned_b, row):
    for half in range(2):
        cut = slice(half * 128, half * 128 + 128)
        turned_a[row, EDGE + half * 128 : EDGE + half * 128 + 128, :] = jnp.transpose(wide[row, 0:128, cut])
    both = jnp.concatenate([wide[row, 128:CA, 0:128], wide[row, 128:CA, 128:256]], axis=0)
    turned_b[row, EDGE : EDGE + 128, :] = jnp.transpose(both)


def turn_sea(values, turned, row):
    for half in range(2):
        cut = slice(half * 128, half * 128 + 128)
        full = jnp.concatenate([values[:, cut], jnp.zeros((128 - CO, 128), F32)], axis=0)
        turned[row, EDGE + half * 128 : EDGE + half * 128 + 128, :] = jnp.transpose(full)


def depthwise(src, taps, tops, rows, cols, out, m, add=False):
    pairs = {row: [t for t in tops if 0 <= row - t < 7] for row in rows}

    def step(g, carry):
        start = g * (8 * m)
        to = [pl.ds(pl.multiple_of(start + 8 * b, 8), 8) for b in range(m)]
        sums = {t: [out[t, to[b], :] if add else jnp.zeros((8, 128), F32) for b in range(m)] for t in tops}
        for j in range(7):
            weights = {i: taps[i * 7 + j] for i in {row - t for row in rows for t in pairs[row]}}
            for row in rows:
                for b in range(m):
                    v = src[row, pl.ds(start + (8 * b + EDGE - 3 + j), 8), :]
                    for t in pairs[row]:
                        sums[t][b] = sums[t][b] + weights[row - t] * v
        for t in tops:
            for b in range(m):
                out[t, to[b], :] = sums[t][b]
        return carry

    lax.fori_loop(0, cols // (8 * m), step, 0)


def ring(value, step, count):
    return lax.rem(value + (step + count), count)


def fused_kernel(
    src, count, atm_hbm, sea_hbm, weights_hbm,
    kernel_atm, w_in_atm, w_out_atm, w_flux, kernel_sea, w_in_sea, w_out_sea, w_couple,
    atm_out, sea_out,
    atm_raw, sea_raw, aw, ata, atb, sw, st,
    a_out, a_in, s_out, s_in, mirror_w, mirror_out, mirror_in,
    taps_a, taps_b, taps_s, conv_a, conv_b, conv_s,
    wi_a, wo_a, wf_a, hidden, wi_s, wo_s, wic_s, pre, blocks, slots, w_cat, back_a, back_s,
    load_sem, slot_sem, out_sem, send_sem, recv_sem, flux_send, flux_recv,
):
    face, tile = lax.axis_index("face"), lax.axis_index("tile")
    up, down = ring(face, 1, N_FACE), ring(face, -1, N_FACE)
    north, south = ring(tile, 1, N_TILE), ring(tile, -1, N_TILE)
    y, x, core = tile // 4, lax.rem(tile // 2, 2), lax.rem(tile, 2)
    top = tile == N_TILE - 1
    across = (N_FACE - 1 - face, tile)

    def at(dy, dx, dc):
        return (ring(y, dy, 4) * 2 + lax.rem(x + dx, 2)) * 2 + lax.rem(core + dc, 2)

    partner, sibling = at(0, 1, 0), at(0, 0, 1)

    loads = []
    for half in range(2):
        cut = pl.ds(128 * half, 128)
        loads.append(pltpu.make_async_copy(atm_hbm.at[:, :, cut], atm_raw.at[half], load_sem.at[half]))
    for half in range(2):
        cut = pl.ds(128 * half, 128)
        loads.append(pltpu.make_async_copy(sea_hbm.at[:, :, cut], sea_raw.at[half], load_sem.at[2 + half]))
    for load in loads:
        load.start()

    def weight_load(n):
        return pltpu.make_async_copy(weights_hbm.at[pl.ds(4 * n, 4)], slots.at[n % 2], slot_sem.at[n % 2])

    weight_load(0).start()
    weight_load(1).start()

    barrier = pltpu.get_barrier_semaphore()
    near = [
        (up, tile), (down, tile), (face, north), (face, south),
        (up, north), (up, south), (down, north), (down, south),
        (face, partner), (face, at(1, 0, 0)), (face, at(-1, 0, 0)), (face, at(2, 0, 0)),
    ]
    for device in near:
        pl.semaphore_signal(barrier, inc=1, device_id=device, device_id_type=MESH)

    @pl.when(top)
    def _():
        pl.semaphore_signal(barrier, inc=1, device_id=across, device_id_type=MESH)

    def copy(k, src_ref, dst_ref, device):
        return pltpu.make_async_remote_copy(
            src_ref=src_ref, dst_ref=dst_ref, send_sem=send_sem.at[k], recv_sem=recv_sem.at[k],
            device_id=device, device_id_type=MESH,
        )

    loads[0].wait()
    loads[1].wait()
    rows_out_of(atm_raw, AR, CA, aw.at[pl.ds(3, AR)])
    pl.semaphore_wait(barrier, len(near) + tile // (N_TILE - 1))
    row_copies = []
    for d in range(3):
        row_copies.append(copy(2 * d, aw.at[10 - d], aw.at[2 - d], (up, tile)))
        row_copies.append(copy(2 * d + 1, aw.at[3 + d], aw.at[11 + d], (down, tile)))
    for c in row_copies[0:2]:
        c.start()

    for r in range(AR):
        turn_atm(aw, ata, atb, 3 + r)
    for r in range(AR):
        to = pl.ds(16 * (r // 4) + 4 * r, 3)
        a_out[0, to, :] = ata[3 + r, pl.ds(EDGE + COLS - 3, 3), :]
        a_out[1, to, :] = ata[3 + r, pl.ds(EDGE, 3), :]
        to = pl.ds(16 * (r // 4) + 4 * r + 16, 3)
        a_out[0, to, :] = swap_halves(atb[3 + r, pl.ds(EDGE + 125, 3), :])
        a_out[1, to, :] = swap_halves(atb[3 + r, pl.ds(EDGE, 3), :])
    edge_copies = []
    for n, f in enumerate((up, face, down)):
        part = (pl.ds(32, 32), pl.ds(0, 64), pl.ds(0, 32))[n]
        edge_copies.append(copy(6 + n, a_out.at[0, part], a_in.at[0, n, part], (f, north)))
        edge_copies.append(copy(9 + n, a_out.at[1, part], a_in.at[1, n, part], (f, south)))
    for n in (2, 3, 0, 1, 4, 5):
        edge_copies[n].start()

    def atm_edges(row):
        n = 0 if row < 3 else 1 if row < 3 + AR else 2
        r = (row - 3) % AR
        low = lax.broadcasted_iota(jnp.int32, (3, 128), 1) < 64
        frm = pl.ds(16 * (r // 4) + 4 * r, 3)
        ata[row, pl.ds(EDGE - 3, 3), :] = a_in[0, n, frm, :]
        ata[row, pl.ds(EDGE + COLS, 3), :] = a_in[1, n, frm, :]
        frm = pl.ds(16 * (r // 4) + 4 * r + 16, 3)
        inner = swap_halves(atb[row, pl.ds(EDGE + 125, 3), :])
        outer = swap_halves(atb[row, pl.ds(EDGE, 3), :])
        atb[row, pl.ds(EDGE - 3, 3), :] = jnp.where(low, a_in[0, n, frm, :], inner)
        atb[row, pl.ds(EDGE + 128, 3), :] = jnp.where(low, outer, a_in[1, n, frm, :])

    for t in range(49):
        k = kernel_atm[t : t + 1, :]
        taps_a[t] = jnp.broadcast_to(k[:, 0:128], (8, 128))
        taps_b[t] = jnp.broadcast_to(jnp.concatenate([k[:, 128:CA], k[:, 128:CA]], axis=1), (8, 128))
    turned = jnp.transpose(w_in_atm[...])
    gap = jnp.zeros((HA, 64), F32)
    for n, full in enumerate(
        (jnp.concatenate([turned, gap], axis=1), jnp.concatenate([turned[:, 0:128], gap, turned[:, 128:CA]], axis=1))
    ):
        hi, lo = split(full)
        for c in range(3):
            wi_a[n, c, 0:256, :] = hi[256 * c : 256 * c + 256]
            wi_a[n, c, 256:512, :] = lo[256 * c : 256 * c + 256]
    wo_a[0:CA, :], wo_a[CA : 2 * CA, :] = split(w_out_atm[...])
    wf_a[0:FL, :], wf_a[FL : 2 * FL, :] = split(w_flux[...])
    depth = lax.broadcasted_iota(jnp.int32, (256, 128), 0)
    lane = lax.broadcasted_iota(jnp.int32, (256, 128), 1)
    ones_first = one_where(depth < CA)
    ones_second = one_where((depth < 128) | (depth >= CA))

    def mm_stacked(stack, size, right):
        both = mm(stack, right[0])
        return both[0:size] + (both[size : 2 * size] + mm(stack[0:size], right[1]))

    def atm_depthwise(tops, rows, m, add):
        depthwise(ata, taps_a, tops, rows, 256, conv_a, m, add)
        depthwise(atb, taps_b, tops, rows, 128, conv_b, m, add)

    def atm_stage(stage):
        tops = STAGES[stage]
        b = jnp.concatenate([conv_b[t] for t in tops], axis=0)
        a1 = jnp.concatenate([conv_a[t, 0:128] for t in tops], axis=0)
        a2 = jnp.concatenate([conv_a[t, 128:256] for t in tops], axis=0)
        m1 = lane_sum(jnp.concatenate([a1, b], axis=1), ones_first, 3) * (1.0 / CA)
        m2 = lane_sum(jnp.concatenate([a2, b], axis=1), ones_second, 3) * (1.0 / CA)
        a1, a2, b = a1 - m1, a2 - m2, b - jnp.where(lane < 64, m1, m2)
        v1 = lane_sum(jnp.concatenate([a1 * a1, b * b], axis=1), ones_first, 2) * (1.0 / CA)
        v2 = lane_sum(jnp.concatenate([a2 * a2, b * b], axis=1), ones_second, 2) * (1.0 / CA)
        r1, r2 = lax.rsqrt(v1 + 1e-06), lax.rsqrt(v2 + 1e-06)
        b = b * jnp.where(lane < 64, r1, r2)
        normed = (
            split(jnp.concatenate([a1 * r1, b], axis=1)),
            split(jnp.concatenate([a2 * r2, b], axis=1)),
        )
        for c in range(3):
            for half in range(2):
                hi, lo = normed[half]
                both = mm_t(wi_a[half, c], hi)
                value = gelu(both[0:256] + (both[256:512] + mm_t(wi_a[half, c, 0:256], lo)))
                to = (slice(256 * c, 256 * c + 256), slice(256 * half, 256 * half + 256))
                hidden[(0, *to)], hidden[(1, *to)] = split(value)
        for half in range(2):
            cut = slice(256 * half, 256 * half + 256)
            mixed = mm_stacked(wo_a[...], CA, (hidden[0, :, cut], hidden[1, :, cut]))
            here = slice(half * 128, half * 128 + 128)
            value = mixed + jnp.concatenate([aw[3 + row, :, here] for row in tops], axis=1)
            flux = mm_stacked(wf_a[...], FL, split(value))
            for n, row in enumerate(tops):
                part = slice(n * 128, n * 128 + 128)
                blocks[tile, 4 * stage + 2 * n + half] = flux[:, part]
                back_a.at[half].reshape(CA * AR, 128)[pl.ds(row, CA, stride=AR), :] = value[:, part]

    def flux_copy(stage, kind, block, target):
        part = blocks.at[block, pl.ds(4 * stage, 4)]
        return pltpu.make_async_remote_copy(
            src_ref=part, dst_ref=part, send_sem=flux_send.at[stage, kind], recv_sem=flux_recv.at[stage, kind],
            device_id=(face, target), device_id_type=MESH,
        )

    sent = []

    def start(*mine):
        for c in mine:
            c.start()
        sent.extend(mine)

    def arrived(stage, kind, block):
        flux_copy(stage, kind, block, partner).wait_recv()

    def send_own(stage):
        start(flux_copy(stage, 0, tile, partner))
        start(flux_copy(stage, 1, tile, at(1, 0, 0)), flux_copy(stage, 2, tile, at(-1, 0, 0)))
        if stage == 3:
            start(flux_copy(stage, 3, tile, at(2, 0, 0)))
        start(flux_copy(stage, 7, tile, sibling))

    def relay(stage):
        arrived(stage, 0, partner)
        start(flux_copy(stage, 4, partner, at(1, 0, 0)), flux_copy(stage, 5, partner, at(-1, 0, 0)))
        if stage == 3:
            start(flux_copy(stage, 6, partner, at(2, 0, 0)))
        start(flux_copy(stage, 8, partner, sibling))

    def near_own(stage):
        arrived(stage, 1, at(-1, 0, 0))
        if stage < 3:
            start(flux_copy(stage, 3, at(-1, 0, 0), at(1, 0, 0)))
        start(flux_copy(stage, 9, at(-1, 0, 0), sibling))
        arrived(stage, 2, at(1, 0, 0))
        start(flux_copy(stage, 10, at(1, 0, 0), sibling))

    def near_relayed(stage):
        arrived(stage, 5, at(1, 1, 0))
        if stage < 3:
            start(flux_copy(stage, 6, at(1, 1, 0), at(-1, 0, 0)))
        start(flux_copy(stage, 13, at(1, 1, 0), sibling))
        arrived(stage, 4, at(-1, 1, 0))
        start(flux_copy(stage, 12, at(-1, 1, 0), sibling))

    def far_own(stage):
        arrived(stage, 3, at(2, 0, 0))
        start(flux_copy(stage, 11, at(2, 0, 0), sibling))

    def far_relayed(stage):
        arrived(stage, 6, at(2, 1, 0))
        start(flux_copy(stage, 14, at(2, 1, 0), sibling))

    def finish(stage):
        arrived(stage, 7, sibling)
        arrived(stage, 8, at(0, 1, 1))
        for hop in range(2):
            arrived(stage, 9 + 3 * hop, at(-1, hop, 1))
            arrived(stage, 10 + 3 * hop, at(1, hop, 1))
            arrived(stage, 11 + 3 * hop, at(2, hop, 1))

    def sea_start():
        loads[2].wait()
        loads[3].wait()
        rows_out_of(sea_raw, OR, CO, sw.at[pl.ds(3, OR)])
        sea_copies = [
            copy(12, sw.at[pl.ds(16, 3)], sw.at[pl.ds(0, 3)], (face, north)),
            copy(13, sw.at[pl.ds(3, 3)], sw.at[pl.ds(19, 3)], (face, south)),
        ]
        for r in range(OR):
            turn_sea(sw[3 + r], st, 3 + r)
        for r in range(OR):
            to = pl.ds(4 * r, 3)
            s_out[0, to, :] = st[3 + r, pl.ds(EDGE + COLS - 3, 3), :]
            s_out[1, to, :] = st[3 + r, pl.ds(EDGE, 3), :]
        for n, t in enumerate((north, tile, south)):
            part = (pl.ds(48, 16), pl.ds(0, 64), pl.ds(0, 16))[n]
            sea_copies.append(copy(14 + n, s_out.at[0, part], s_in.at[0, n, part], (up, t)))
            sea_copies.append(copy(17 + n, s_out.at[1, part], s_in.at[1, n, part], (down, t)))
        for c in sea_copies[2:]:
            c.start()
        return sea_copies

    sea_copies = sea_start()

    for n in (2, 3):
        edge_copies[n].wait_recv()
    for r in range(AR):
        atm_edges(3 + r)
    own = tuple(range(3, 3 + AR))
    atm_depthwise((3, 4), own, 4, False)
    atm_stage(0)
    send_own(0)
    for c in row_copies[2:4]:
        c.start()

    def sea_parameters():
        for t in range(49):
            k = jnp.concatenate([kernel_sea[t : t + 1, :], jnp.zeros((1, 128 - CO), F32)], axis=1)
            taps_s[t] = jnp.broadcast_to(k, (8, 128))
        hi, lo = split(jnp.concatenate([w_in_sea[...], jnp.zeros((128 - CO, HO), F32)], axis=0))
        wi_s[0:128] = hi
        wi_s[128:256] = hi
        wi_s[256:384] = lo
        blank = jnp.zeros((HO, 128 - CO), F32)
        hi, lo = split(jnp.concatenate([jnp.transpose(w_out_sea[...]), blank], axis=1))
        wo_s[0:HO, 0:128] = hi
        wo_s[0:HO, 128:256] = lo
        wo_s[HO : 2 * HO, 0:128] = hi
        wo_s[HO : 2 * HO, 128:256] = jnp.zeros((HO, 128), BF16)
        left, right = split(w_couple[...]), split(w_in_sea[...])
        hi, lo = split(mm(left[0], right[0]) + (mm(left[1], right[0]) + mm(left[0], right[1])))
        wic_s[0:FL] = hi
        wic_s[FL : 2 * FL] = hi
        wic_s[2 * FL : 3 * FL] = lo
        wic_s[3 * FL : 4 * FL] = jnp.zeros((FL, HO), BF16)

    ones_sea = one_where(depth[0:128] < CO)

    def sea_edges(row, n, r):
        frm = pl.ds(4 * r, 3)
        st[row, pl.ds(EDGE - 3, 3), :] = s_in[0, n, frm, :]
        st[row, pl.ds(EDGE + COLS, 3), :] = s_in[1, n, frm, :]

    def sea_piece(piece):
        first, end = PIECES[piece]
        size = (end - first) * COLS
        c = conv_s[first:end].reshape(size, 128)
        c = c - lane_sum(c, ones_sea, 3) * (1.0 / CO)
        spread = lane_sum(c * c, ones_sea, 2) * (1.0 / CO)
        hi, lo = split(c * lax.rsqrt(spread + 1e-06))
        value = mm(jnp.concatenate([hi, lo], axis=1), wi_s[0:256]) + mm(hi, wi_s[256:384])
        pre[first:end] = value.reshape(end - first, COLS, HO)

    def sea_depthwise(tops, rows, add=False):
        depthwise(st, taps_s, tops, rows, COLS, conv_s, 2, add)

    def split_weights(n):
        weight_load(n).wait()

        def step(b, carry):
            w_cat[4 * n + b, :, 0:128], w_cat[4 * n + b, :, 128:256] = split(slots[n % 2, b].reshape(512, 128))
            return carry

        lax.fori_loop(0, 4, step, 0)
        if n + 2 < 8:
            weight_load(n + 2).start()

    def atm_rows(d):
        row_copies[2 * d].wait_recv()
        row_copies[2 * d + 1].wait_recv()
        if d == 0:
            for n in (0, 1, 4, 5):
                edge_copies[n].wait_recv()
        for row in (2 - d, 11 + d):
            turn_atm(aw, ata, atb, row)
            atm_edges(row)

    def atm_halo(d):
        atm_rows(d)
        tops = tuple(range(3 - d)) + tuple(range(5 + d, AR))
        atm_depthwise(tops, (2 - d, 11 + d), 2 if d == 0 else 4, True)

    atm_depthwise((0, 1, 2, 5, 6, 7), own, 2, False)
    split_weights(0)
    atm_halo(0)
    atm_stage(1)
    send_own(1)
    for c in row_copies[4:6]:
        c.start()
    for c in sea_copies[:2]:
        c.start()
    relay(0)
    near_own(0)
    sea_parameters()
    for n in (2, 3):
        sea_copies[2 + n].wait_recv()
    for r in range(OR):
        sea_edges(3 + r, 1, r)
    sea_depthwise((3, 4, 5, 6, 7), tuple(range(3, 14)))
    split_weights(1)
    atm_halo(1)
    atm_stage(2)
    send_own(2)
    relay(1)
    near_relayed(0)
    near_own(1)

    fold = [
        copy(20, sw.at[pl.ds(16, 3)], mirror_w, across),
        copy(21, mirror_out, mirror_in, across),
    ]

    @pl.when(top)
    def _():
        for r in range(3):
            mirror_out[pl.ds(8 * r, 3), :] = st[16 + r, pl.ds(EDGE - 3, 3), :]
            mirror_out[pl.ds(8 * r + 4, 3), :] = st[16 + r, pl.ds(EDGE + COLS, 3), :]
        for c in fold:
            c.start()

    split_weights(2)
    far_own(0)
    sea_depthwise((8, 9, 10, 11, 12), tuple(range(8, 19)))
    sea_piece(0)
    split_weights(3)
    near_relayed(1)
    far_own(1)
    far_relayed(0)
    atm_halo(2)
    atm_stage(3)
    send_own(3)
    relay(2)
    atm_store = []
    for half in range(2):
        cut = pl.ds(128 * half, 128)
        atm_store.append(pltpu.make_async_copy(back_a.at[half], atm_out.at[:, :, cut], out_sem.at[half]))
    for c in atm_store:
        c.start()
    near_own(2)
    split_weights(4)
    split_weights(5)
    relay(3)
    split_weights(6)
    near_own(3)
    near_relayed(2)
    far_own(2)
    far_relayed(1)
    sea_piece(1)
    split_weights(7)
    sea_depthwise((0, 1, 2), tuple(range(3, 9)))
    sea_depthwise((13, 14, 15), tuple(range(13, 19)))
    near_relayed(3)
    far_own(3)
    far_relayed(2)
    far_relayed(3)

    for n in (0, 1, 4, 5):
        sea_copies[2 + n].wait_recv()
    for c in sea_copies[:2]:
        c.wait_recv()
    for r in range(3):
        turn_sea(sw[r], st, r)
        sea_edges(r, 0, OR - 3 + r)
        turn_sea(sw[3 + OR + r], st, 3 + OR + r)
        sea_edges(3 + OR + r, 2, r)

    @pl.when(tile == 0)
    def _():
        st[0:3] = jnp.zeros((3, COLS + 2 * EDGE, 128), F32)

    @pl.when(top)
    def _():
        for c in fold:
            c.wait()
        flip = 127 - lax.broadcasted_iota(jnp.int32, (CO, 128), 1)
        for k in range(3):
            first = jnp.take_along_axis(mirror_w[2 - k, :, 128:256], flip, axis=1)
            second = jnp.take_along_axis(mirror_w[2 - k, :, 0:128], flip, axis=1)
            turn_sea(jnp.concatenate([first, second], axis=1), st, 19 + k)
            for c in range(3):
                st[19 + k, pl.ds(EDGE - 3 + c, 1), :] = mirror_in[pl.ds(8 * (2 - k) + 4 + 2 - c, 1), :]
                st[19 + k, pl.ds(EDGE + COLS + c, 1), :] = mirror_in[pl.ds(8 * (2 - k) + 2 - c, 1), :]

    sea_depthwise((0, 1, 2), (0, 1, 2), True)
    sea_depthwise((13, 14, 15), (19, 20, 21), True)
    sea_piece(2)
    sea_piece(3)
    for stage in range(4):
        finish(stage)

    def flux_of(block):
        live = count[block]
        picked = []
        for k in range(4):
            index = src[k, block]
            t, a = index // 16, lax.rem(index, 16)
            r = a // 2
            spot = jnp.where(r < 4, (3 - r) * 4, (r - 4) * 4 + 2) + lax.rem(a, 2)
            picked.append(jnp.where(k < live, blocks[t, spot], 0.0))
        hi, lo = split(jnp.concatenate(picked, axis=1))
        both = mm(jnp.concatenate([hi, lo], axis=0), w_cat[block])
        flux = both[0:FL, 0:128] + (both[0:FL, 128:256] + both[FL : 2 * FL, 0:128])
        hi = flux.astype(BF16).astype(F32)
        turned = jnp.transpose(jnp.concatenate([hi, flux - hi], axis=0)).astype(BF16)
        return jnp.concatenate([turned, turned], axis=1)

    def sea_rows(q, n):
        flux = jnp.concatenate([flux_of(2 * q + i) for i in range(2 * n)], axis=0)
        grown = gelu(pre[pl.ds(q, n)].reshape(n * COLS, HO) + mm(flux, wic_s[...]))
        out = mm(jnp.concatenate(split(grown), axis=1), wo_s[...])
        out = out[:, 0:128] + out[:, 128:256]
        for i in range(n):
            for half in range(2):
                at_cell = i * COLS + half * 128
                value = jnp.transpose(out[at_cell : at_cell + 128])[0:CO]
                value = value + sw[3 + q + i, :, half * 128 : half * 128 + 128]
                back_s.at[half].reshape(CO * OR, 128)[pl.ds(q + i, CO, stride=OR), :] = value

    sea_store = []
    for part in range(2):

        def step(i, carry, part=part):
            sea_rows(8 * part + 4 * i, 2)
            sea_rows(8 * part + 4 * i + 2, 2)
            return carry

        lax.fori_loop(0, 2, step, 0)
        for half in range(2):
            rows, cut = pl.ds(8 * part, 8), pl.ds(128 * half, 128)
            c = pltpu.make_async_copy(
                back_s.at[half, :, rows], sea_out.at[:, rows, cut], out_sem.at[2 + 2 * part + half]
            )
            c.start()
            sea_store.append(c)
    for c in row_copies + edge_copies + sea_copies + sent:
        c.wait_send()
    for c in atm_store + sea_store:
        c.wait()


def step(src, count, atmosphere, ocean, weights, *params):
    return pl.pallas_call(
        fused_kernel,
        out_shape=(
            jax.ShapeDtypeStruct((CA, AR, COLS), F32),
            jax.ShapeDtypeStruct((CO, OR, COLS), F32),
        ),
        in_specs=[SMEM, SMEM, ANY, ANY, ANY] + [VMEM] * 8,
        out_specs=(ANY, ANY),
        scratch_shapes=[
            pltpu.VMEM((2, CA, AR, 128), F32),
            pltpu.VMEM((2, CO, OR, 128), F32),
            pltpu.VMEM((AR + 6, CA, COLS), F32),
            pltpu.VMEM((AR + 6, COLS + 2 * EDGE, 128), F32),
            pltpu.VMEM((AR + 6, 128 + 2 * EDGE, 128), F32),
            pltpu.VMEM((OR + 6, CO, COLS), F32),
            pltpu.VMEM((OR + 6, COLS + 2 * EDGE, 128), F32),
            pltpu.VMEM((2, 64, 128), F32),
            pltpu.VMEM((2, 3, 64, 128), F32),
            pltpu.VMEM((2, 64, 128), F32),
            pltpu.VMEM((2, 3, 64, 128), F32),
            pltpu.VMEM((3, CO, COLS), F32),
            pltpu.VMEM((24, 128), F32),
            pltpu.VMEM((24, 128), F32),
            pltpu.VMEM((49, 8, 128), F32),
            pltpu.VMEM((49, 8, 128), F32),
            pltpu.VMEM((49, 8, 128), F32),
            pltpu.VMEM((AR, 256, 128), F32),
            pltpu.VMEM((AR, 128, 128), F32),
            pltpu.VMEM((OR, 256, 128), F32),
            pltpu.VMEM((2, 3, 512, 256), BF16),
            pltpu.VMEM((2 * CA, HA), BF16),
            pltpu.VMEM((2 * FL, CA), BF16),
            pltpu.VMEM((2, HA, 2 * COLS), BF16),
            pltpu.VMEM((384, HO), BF16),
            pltpu.VMEM((2 * HO, 256), BF16),
            pltpu.VMEM((4 * FL, HO), BF16),
            pltpu.VMEM((OR, COLS, HO), F32),
            pltpu.VMEM((N_TILE, 16, FL, 128), F32),
            pltpu.VMEM((2, 4, 4, 128, 128), F32),
            pltpu.VMEM((32, 512, 256), BF16),
            pltpu.VMEM((2, CA, AR, 128), F32),
            pltpu.VMEM((2, CO, OR, 128), F32),
            DMA((4,)),
            DMA((2,)),
            DMA((6,)),
            DMA((22,)),
            DMA((22,)),
            DMA((4, 15)),
            DMA((4, 15)),
        ],
        compiler_params=pltpu.CompilerParams(
            collective_id=0, has_side_effects=True, vmem_limit_bytes=57 * MIB
        ),
        name="coupled",
    )(src, count, atmosphere, ocean, weights, *params)


def hand_over_kernel(atm, sea, atm_out, sea_out):
    atm_out[...] = atm[...]
    sea_out[...] = sea[...]


def hand_over(atm, sea):
    cut = lambda channels, rows: pl.BlockSpec((channels // 4, rows, COLS), lambda i: (i, 0, 0))
    return pl.pallas_call(
        hand_over_kernel,
        grid=(4,),
        out_shape=(
            jax.ShapeDtypeStruct((CA, AR, COLS), F32),
            jax.ShapeDtypeStruct((CO, OR, COLS), F32),
        ),
        in_specs=[cut(CA, AR), cut(CO, OR)],
        out_specs=(cut(CA, AR), cut(CO, OR)),
        name="hand_over",
    )(atm, sea)


def body(
    atmosphere, ocean, kernel_atm, w_in_atm, w_out_atm, w_flux, kernel_ocean, w_in_ocean,
    w_out_ocean, w_couple, intersection_src, intersection_count, intersection_weight,
):
    results = step(
        intersection_src[0].T, intersection_count[0], atmosphere, ocean, intersection_weight[0],
        kernel_atm.T, w_in_atm, w_out_atm, w_flux, kernel_ocean.T, w_in_ocean, w_out_ocean, w_couple.T,
    )
    return hand_over(*results)


def solution(mesh):
    return jax.shard_map(
        body,
        mesh=mesh,
        in_specs=(
            P(None, "face", "tile"),
            P(None, "tile", "face"),
            P(), P(), P(), P(), P(), P(), P(), P(),
            P("face", "tile", None),
            P("face", "tile"),
            P("face", "tile", None, None, None),
        ),
        out_specs=(P(None, "face", "tile"), P(None, "tile", "face")),
        check_vma=False,
    )
```

```python
import jax
import jax.numpy as jnp
from jax import lax
from jax.experimental import pallas as pl
from jax.experimental.pallas import tpu as pltpu
from jax.sharding import PartitionSpec as P

F32 = jnp.float32
BF16 = jnp.bfloat16
MESH = pl.DeviceIdType.MESH
MIB = 2**20
VMEM = pl.BlockSpec(memory_space=pltpu.VMEM)
SMEM = pl.BlockSpec(memory_space=pltpu.SMEM)
ANY = pl.BlockSpec(memory_space=pl.ANY)
DMA = pltpu.SemaphoreType.DMA

CA, HA, CO, HO, FL = 192, 768, 96, 384, 64
AR, OR, COLS = 8, 16, 256
N_FACE, N_TILE = 8, 16
EDGE = 8
STAGES = ((3, 4), (2, 5), (1, 6), (0, 7))
PIECES = ((3, 8), (8, 13), (0, 3), (13, 16))


def split(x):
    hi = x.astype(BF16)
    return hi, (x - hi.astype(F32)).astype(BF16)


def mm(a, b):
    return jnp.dot(a, b, preferred_element_type=F32)


def mm_t(a, b):
    return lax.dot_general(a, b, (((1,), (1,)), ((), ())), preferred_element_type=F32)


def gelu(x):
    return 0.5 * x * (1.0 + lax.erf(x * 0.7071067811865476))


def lane_sum(x, ones, parts):
    total = 0.0
    for _ in range(parts):
        part = x.astype(BF16)
        x = x - part.astype(F32)
        total = total + mm(part, ones)
    return total


def one_where(condition):
    return jnp.where(condition, 1.0, 0.0).astype(BF16)


def swap_halves(x):
    return pltpu.roll(x, 64, 1)


def rows_out_of(raw, rows, channels, wide):
    for half in range(2):
        flat = raw.at[half].reshape(channels * rows, 128)
        for r in range(rows):
            wide[r, :, half * 128 : half * 128 + 128] = flat[pl.ds(r, channels, stride=rows), :]


def turn_atm(wide, turned_a, turned_b, row):
    for half in range(2):
        cut = slice(half * 128, half * 128 + 128)
        turned_a[row, EDGE + half * 128 : EDGE + half * 128 + 128, :] = jnp.transpose(wide[row, 0:128, cut])
    both = jnp.concatenate([wide[row, 128:CA, 0:128], wide[row, 128:CA, 128:256]], axis=0)
    turned_b[row, EDGE : EDGE + 128, :] = jnp.transpose(both)


def turn_sea(values, turned, row):
    for half in range(2):
        cut = slice(half * 128, half * 128 + 128)
        full = jnp.concatenate([values[:, cut], jnp.zeros((128 - CO, 128), F32)], axis=0)
        turned[row, EDGE + half * 128 : EDGE + half * 128 + 128, :] = jnp.transpose(full)


def depthwise(src, taps, tops, rows, cols, out, m, add=False):
    pairs = {row: [t for t in tops if 0 <= row - t < 7] for row in rows}

    def step(g, carry):
        start = g * (8 * m)
        to = [pl.ds(pl.multiple_of(start + 8 * b, 8), 8) for b in range(m)]
        sums = {t: [out[t, to[b], :] if add else jnp.zeros((8, 128), F32) for b in range(m)] for t in tops}
        for j in range(7):
            weights = {i: taps[i * 7 + j] for i in {row - t for row in rows for t in pairs[row]}}
            for row in rows:
                for b in range(m):
                    v = src[row, pl.ds(start + (8 * b + EDGE - 3 + j), 8), :]
                    for t in pairs[row]:
                        sums[t][b] = sums[t][b] + weights[row - t] * v
        for t in tops:
            for b in range(m):
                out[t, to[b], :] = sums[t][b]
        return carry

    lax.fori_loop(0, cols // (8 * m), step, 0)


def ring(value, step, count):
    return lax.rem(value + (step + count), count)


def fused_kernel(
    src, count, atm_hbm, sea_hbm, weights_hbm,
    kernel_atm, w_in_atm, w_out_atm, w_flux, kernel_sea, w_in_sea, w_out_sea, w_couple,
    atm_out, sea_out,
    atm_raw, sea_raw, aw, ata, atb, sw, st,
    a_out, a_in, s_out, s_in, mirror_w, mirror_out, mirror_in,
    taps_a, taps_b, taps_s, conv_a, conv_b, conv_s,
    wi_a, wo_a, wf_a, hidden, wi_s, wo_s, wic_s, pre, blocks, slots, w_cat, back_a, back_s,
    load_sem, slot_sem, out_sem, send_sem, recv_sem, flux_send, flux_recv,
):
    face, tile = lax.axis_index("face"), lax.axis_index("tile")
    up, down = ring(face, 1, N_FACE), ring(face, -1, N_FACE)
    north, south = ring(tile, 1, N_TILE), ring(tile, -1, N_TILE)
    y, x, core = tile // 4, lax.rem(tile // 2, 2), lax.rem(tile, 2)
    top = tile == N_TILE - 1
    across = (N_FACE - 1 - face, tile)

    def at(dy, dx, dc):
        return (ring(y, dy, 4) * 2 + lax.rem(x + dx, 2)) * 2 + lax.rem(core + dc, 2)

    partner, sibling = at(0, 1, 0), at(0, 0, 1)

    loads = []
    for half in range(2):
        cut = pl.ds(128 * half, 128)
        loads.append(pltpu.make_async_copy(atm_hbm.at[:, :, cut], atm_raw.at[half], load_sem.at[half]))
    for half in range(2):
        cut = pl.ds(128 * half, 128)
        loads.append(pltpu.make_async_copy(sea_hbm.at[:, :, cut], sea_raw.at[half], load_sem.at[2 + half]))
    for load in loads:
        load.start()

    def weight_load(n):
        return pltpu.make_async_copy(weights_hbm.at[pl.ds(4 * n, 4)], slots.at[n % 2], slot_sem.at[n % 2])

    weight_load(0).start()
    weight_load(1).start()

    barrier = pltpu.get_barrier_semaphore()
    near = [
        (up, tile), (down, tile), (face, north), (face, south),
        (up, north), (up, south), (down, north), (down, south),
        (face, partner), (face, at(1, 0, 0)), (face, at(-1, 0, 0)), (face, at(2, 0, 0)),
    ]
    for device in near:
        pl.semaphore_signal(barrier, inc=1, device_id=device, device_id_type=MESH)

    @pl.when(top)
    def _():
        pl.semaphore_signal(barrier, inc=1, device_id=across, device_id_type=MESH)

    def copy(k, src_ref, dst_ref, device):
        return pltpu.make_async_remote_copy(
            src_ref=src_ref, dst_ref=dst_ref, send_sem=send_sem.at[k], recv_sem=recv_sem.at[k],
            device_id=device, device_id_type=MESH,
        )

    loads[0].wait()
    loads[1].wait()
    rows_out_of(atm_raw, AR, CA, aw.at[pl.ds(3, AR)])
    row_copies = []
    for d in range(3):
        row_copies.append(copy(2 * d, aw.at[10 - d], aw.at[2 - d], (up, tile)))
        row_copies.append(copy(2 * d + 1, aw.at[3 + d], aw.at[11 + d], (down, tile)))

    for r in range(AR):
        turn_atm(aw, ata, atb, 3 + r)
    for r in range(AR):
        to = pl.ds(16 * (r // 4) + 4 * r, 3)
        a_out[0, to, :] = ata[3 + r, pl.ds(EDGE + COLS - 3, 3), :]
        a_out[1, to, :] = ata[3 + r, pl.ds(EDGE, 3), :]
        to = pl.ds(16 * (r // 4) + 4 * r + 16, 3)
        a_out[0, to, :] = swap_halves(atb[3 + r, pl.ds(EDGE + 125, 3), :])
        a_out[1, to, :] = swap_halves(atb[3 + r, pl.ds(EDGE, 3), :])
    pl.semaphore_wait(barrier, len(near) + tile // (N_TILE - 1))
    edge_copies = []
    for n, f in enumerate((up, face, down)):
        part = (pl.ds(32, 32), pl.ds(0, 64), pl.ds(0, 32))[n]
        edge_copies.append(copy(6 + n, a_out.at[0, part], a_in.at[0, n, part], (f, north)))
        edge_copies.append(copy(9 + n, a_out.at[1, part], a_in.at[1, n, part], (f, south)))
    for n in (2, 3, 0, 1, 4, 5):
        edge_copies[n].start()
    for c in row_copies[0:2]:
        c.start()

    def atm_edges(row):
        n = 0 if row < 3 else 1 if row < 3 + AR else 2
        r = (row - 3) % AR
        low = lax.broadcasted_iota(jnp.int32, (3, 128), 1) < 64
        frm = pl.ds(16 * (r // 4) + 4 * r, 3)
        ata[row, pl.ds(EDGE - 3, 3), :] = a_in[0, n, frm, :]
        ata[row, pl.ds(EDGE + COLS, 3), :] = a_in[1, n, frm, :]
        frm = pl.ds(16 * (r // 4) + 4 * r + 16, 3)
        inner = swap_halves(atb[row, pl.ds(EDGE + 125, 3), :])
        outer = swap_halves(atb[row, pl.ds(EDGE, 3), :])
        atb[row, pl.ds(EDGE - 3, 3), :] = jnp.where(low, a_in[0, n, frm, :], inner)
        atb[row, pl.ds(EDGE + 128, 3), :] = jnp.where(low, outer, a_in[1, n, frm, :])

    for t in range(49):
        k = kernel_atm[t : t + 1, :]
        taps_a[t] = jnp.broadcast_to(k[:, 0:128], (8, 128))
        taps_b[t] = jnp.broadcast_to(jnp.concatenate([k[:, 128:CA], k[:, 128:CA]], axis=1), (8, 128))
    turned = jnp.transpose(w_in_atm[...])
    gap = jnp.zeros((HA, 64), F32)
    for n, full in enumerate(
        (jnp.concatenate([turned, gap], axis=1), jnp.concatenate([turned[:, 0:128], gap, turned[:, 128:CA]], axis=1))
    ):
        hi, lo = split(full)
        for c in range(3):
            wi_a[n, c, 0:256, :] = hi[256 * c : 256 * c + 256]
            wi_a[n, c, 256:512, :] = lo[256 * c : 256 * c + 256]
    wo_a[0:CA, :], wo_a[CA : 2 * CA, :] = split(w_out_atm[...])
    wf_a[0:FL, :], wf_a[FL : 2 * FL, :] = split(w_flux[...])
    depth = lax.broadcasted_iota(jnp.int32, (256, 128), 0)
    lane = lax.broadcasted_iota(jnp.int32, (256, 128), 1)
    ones_first = one_where(depth < CA)
    ones_second = one_where((depth < 128) | (depth >= CA))

    def mm_stacked(stack, size, right):
        both = mm(stack, right[0])
        return both[0:size] + (both[size : 2 * size] + mm(stack[0:size], right[1]))

    def atm_depthwise(tops, rows, m, add):
        depthwise(ata, taps_a, tops, rows, 256, conv_a, m, add)
        depthwise(atb, taps_b, tops, rows, 128, conv_b, m, add)

    def atm_stage(stage):
        tops = STAGES[stage]
        b = jnp.concatenate([conv_b[t] for t in tops], axis=0)
        a1 = jnp.concatenate([conv_a[t, 0:128] for t in tops], axis=0)
        a2 = jnp.concatenate([conv_a[t, 128:256] for t in tops], axis=0)
        m1 = lane_sum(jnp.concatenate([a1, b], axis=1), ones_first, 3) * (1.0 / CA)
        m2 = lane_sum(jnp.concatenate([a2, b], axis=1), ones_second, 3) * (1.0 / CA)
        a1, a2, b = a1 - m1, a2 - m2, b - jnp.where(lane < 64, m1, m2)
        v1 = lane_sum(jnp.concatenate([a1 * a1, b * b], axis=1), ones_first, 2) * (1.0 / CA)
        v2 = lane_sum(jnp.concatenate([a2 * a2, b * b], axis=1), ones_second, 2) * (1.0 / CA)
        r1, r2 = lax.rsqrt(v1 + 1e-06), lax.rsqrt(v2 + 1e-06)
        b = b * jnp.where(lane < 64, r1, r2)
        normed = (
            split(jnp.concatenate([a1 * r1, b], axis=1)),
            split(jnp.concatenate([a2 * r2, b], axis=1)),
        )
        for c in range(3):
            for half in range(2):
                hi, lo = normed[half]
                both = mm_t(wi_a[half, c], hi)
                value = gelu(both[0:256] + (both[256:512] + mm_t(wi_a[half, c, 0:256], lo)))
                to = (slice(256 * c, 256 * c + 256), slice(256 * half, 256 * half + 256))
                hidden[(0, *to)], hidden[(1, *to)] = split(value)
        for half in range(2):
            cut = slice(256 * half, 256 * half + 256)
            mixed = mm_stacked(wo_a[...], CA, (hidden[0, :, cut], hidden[1, :, cut]))
            here = slice(half * 128, half * 128 + 128)
            value = mixed + jnp.concatenate([aw[3 + row, :, here] for row in tops], axis=1)
            flux = mm_stacked(wf_a[...], FL, split(value))
            for n, row in enumerate(tops):
                part = slice(n * 128, n * 128 + 128)
                blocks[tile, 4 * stage + 2 * n + half] = flux[:, part]
                back_a.at[half].reshape(CA * AR, 128)[pl.ds(row, CA, stride=AR), :] = value[:, part]

    def flux_copy(stage, kind, block, target):
        part = blocks.at[block, pl.ds(4 * stage, 4)]
        return pltpu.make_async_remote_copy(
            src_ref=part, dst_ref=part, send_sem=flux_send.at[stage, kind], recv_sem=flux_recv.at[stage, kind],
            device_id=(face, target), device_id_type=MESH,
        )

    sent = []

    def start(*mine):
        for c in mine:
            c.start()
        sent.extend(mine)

    def arrived(stage, kind, block):
        flux_copy(stage, kind, block, partner).wait_recv()

    def send_own(stage):
        start(flux_copy(stage, 0, tile, partner))
        start(flux_copy(stage, 1, tile, at(1, 0, 0)), flux_copy(stage, 2, tile, at(-1, 0, 0)))
        if stage == 3:
            start(flux_copy(stage, 3, tile, at(2, 0, 0)))
        start(flux_copy(stage, 7, tile, sibling))

    def relay(stage):
        arrived(stage, 0, partner)
        start(flux_copy(stage, 4, partner, at(1, 0, 0)), flux_copy(stage, 5, partner, at(-1, 0, 0)))
        if stage == 3:
            start(flux_copy(stage, 6, partner, at(2, 0, 0)))
        start(flux_copy(stage, 8, partner, sibling))

    def near_own(stage):
        arrived(stage, 1, at(-1, 0, 0))
        if stage < 3:
            start(flux_copy(stage, 3, at(-1, 0, 0), at(1, 0, 0)))
        start(flux_copy(stage, 9, at(-1, 0, 0), sibling))
        arrived(stage, 2, at(1, 0, 0))
        start(flux_copy(stage, 10, at(1, 0, 0), sibling))

    def near_relayed(stage):
        arrived(stage, 5, at(1, 1, 0))
        if stage < 3:
            start(flux_copy(stage, 6, at(1, 1, 0), at(-1, 0, 0)))
        start(flux_copy(stage, 13, at(1, 1, 0), sibling))
        arrived(stage, 4, at(-1, 1, 0))
        start(flux_copy(stage, 12, at(-1, 1, 0), sibling))

    def far_own(stage):
        arrived(stage, 3, at(2, 0, 0))
        start(flux_copy(stage, 11, at(2, 0, 0), sibling))

    def far_relayed(stage):
        arrived(stage, 6, at(2, 1, 0))
        start(flux_copy(stage, 14, at(2, 1, 0), sibling))

    def finish(stage):
        arrived(stage, 7, sibling)
        arrived(stage, 8, at(0, 1, 1))
        for hop in range(2):
            arrived(stage, 9 + 3 * hop, at(-1, hop, 1))
            arrived(stage, 10 + 3 * hop, at(1, hop, 1))
            arrived(stage, 11 + 3 * hop, at(2, hop, 1))

    def sea_start():
        loads[2].wait()
        loads[3].wait()
        rows_out_of(sea_raw, OR, CO, sw.at[pl.ds(3, OR)])
        sea_copies = [
            copy(12, sw.at[pl.ds(16, 3)], sw.at[pl.ds(0, 3)], (face, north)),
            copy(13, sw.at[pl.ds(3, 3)], sw.at[pl.ds(19, 3)], (face, south)),
        ]
        for r in range(OR):
            turn_sea(sw[3 + r], st, 3 + r)
        for r in range(OR):
            to = pl.ds(4 * r, 3)
            s_out[0, to, :] = st[3 + r, pl.ds(EDGE + COLS - 3, 3), :]
            s_out[1, to, :] = st[3 + r, pl.ds(EDGE, 3), :]
        for n, t in enumerate((north, tile, south)):
            part = (pl.ds(48, 16), pl.ds(0, 64), pl.ds(0, 16))[n]
            sea_copies.append(copy(14 + n, s_out.at[0, part], s_in.at[0, n, part], (up, t)))
            sea_copies.append(copy(17 + n, s_out.at[1, part], s_in.at[1, n, part], (down, t)))
        for c in sea_copies[2:]:
            c.start()
        return sea_copies

    for n in (2, 3):
        edge_copies[n].wait_recv()
    for r in range(AR):
        atm_edges(3 + r)
    own = tuple(range(3, 3 + AR))
    atm_depthwise((3, 4), own, 4, False)
    atm_stage(0)
    send_own(0)
    sea_copies = sea_start()
    for c in row_copies[2:4]:
        c.start()

    def sea_parameters():
        for t in range(49):
            k = jnp.concatenate([kernel_sea[t : t + 1, :], jnp.zeros((1, 128 - CO), F32)], axis=1)
            taps_s[t] = jnp.broadcast_to(k, (8, 128))
        hi, lo = split(jnp.concatenate([w_in_sea[...], jnp.zeros((128 - CO, HO), F32)], axis=0))
        wi_s[0:128] = hi
        wi_s[128:256] = hi
        wi_s[256:384] = lo
        blank = jnp.zeros((HO, 128 - CO), F32)
        hi, lo = split(jnp.concatenate([jnp.transpose(w_out_sea[...]), blank], axis=1))
        wo_s[0:HO, 0:128] = hi
        wo_s[0:HO, 128:256] = lo
        wo_s[HO : 2 * HO, 0:128] = hi
        wo_s[HO : 2 * HO, 128:256] = jnp.zeros((HO, 128), BF16)
        left, right = split(w_couple[...]), split(w_in_sea[...])
        hi, lo = split(mm(left[0], right[0]) + (mm(left[1], right[0]) + mm(left[0], right[1])))
        wic_s[0:FL] = hi
        wic_s[FL : 2 * FL] = hi
        wic_s[2 * FL : 3 * FL] = lo
        wic_s[3 * FL : 4 * FL] = jnp.zeros((FL, HO), BF16)

    ones_sea = one_where(depth[0:128] < CO)

    def sea_edges(row, n, r):
        frm = pl.ds(4 * r, 3)
        st[row, pl.ds(EDGE - 3, 3), :] = s_in[0, n, frm, :]
        st[row, pl.ds(EDGE + COLS, 3), :] = s_in[1, n, frm, :]

    def sea_piece(piece):
        first, end = PIECES[piece]
        size = (end - first) * COLS
        c = conv_s[first:end].reshape(size, 128)
        c = c - lane_sum(c, ones_sea, 3) * (1.0 / CO)
        spread = lane_sum(c * c, ones_sea, 2) * (1.0 / CO)
        hi, lo = split(c * lax.rsqrt(spread + 1e-06))
        value = mm(jnp.concatenate([hi, lo], axis=1), wi_s[0:256]) + mm(hi, wi_s[256:384])
        pre[first:end] = value.reshape(end - first, COLS, HO)

    def sea_depthwise(tops, rows, add=False):
        depthwise(st, taps_s, tops, rows, COLS, conv_s, 2, add)

    def split_weights(n):
        weight_load(n).wait()

        def step(b, carry):
            w_cat[4 * n + b, :, 0:128], w_cat[4 * n + b, :, 128:256] = split(slots[n % 2, b].reshape(512, 128))
            return carry

        lax.fori_loop(0, 4, step, 0)
        if n + 2 < 8:
            weight_load(n + 2).start()

    def atm_rows(d):
        row_copies[2 * d].wait_recv()
        row_copies[2 * d + 1].wait_recv()
        if d == 0:
            for n in (0, 1, 4, 5):
                edge_copies[n].wait_recv()
        for row in (2 - d, 11 + d):
            turn_atm(aw, ata, atb, row)
            atm_edges(row)

    def atm_halo(d):
        atm_rows(d)
        tops = tuple(range(3 - d)) + tuple(range(5 + d, AR))
        atm_depthwise(tops, (2 - d, 11 + d), 2 if d == 0 else 4, True)

    atm_depthwise((0, 1, 2, 5, 6, 7), own, 2, False)
    split_weights(0)
    atm_halo(0)
    atm_stage(1)
    send_own(1)
    for c in row_copies[4:6]:
        c.start()
    for c in sea_copies[:2]:
        c.start()
    relay(0)
    near_own(0)
    sea_parameters()
    for n in (2, 3):
        sea_copies[2 + n].wait_recv()
    for r in range(OR):
        sea_edges(3 + r, 1, r)
    sea_depthwise((3, 4, 5, 6, 7), tuple(range(3, 14)))
    split_weights(1)
    atm_halo(1)
    atm_stage(2)
    send_own(2)
    relay(1)
    near_relayed(0)
    near_own(1)

    fold = [
        copy(20, sw.at[pl.ds(16, 3)], mirror_w, across),
        copy(21, mirror_out, mirror_in, across),
    ]

    @pl.when(top)
    def _():
        for r in range(3):
            mirror_out[pl.ds(8 * r, 3), :] = st[16 + r, pl.ds(EDGE - 3, 3), :]
            mirror_out[pl.ds(8 * r + 4, 3), :] = st[16 + r, pl.ds(EDGE + COLS, 3), :]
        for c in fold:
            c.start()

    split_weights(2)
    far_own(0)
    sea_depthwise((8, 9, 10, 11, 12), tuple(range(8, 19)))
    sea_piece(0)
    split_weights(3)
    near_relayed(1)
    far_own(1)
    far_relayed(0)
    atm_halo(2)
    atm_stage(3)
    send_own(3)
    atm_store = []
    for half in range(2):
        cut = pl.ds(128 * half, 128)
        atm_store.append(pltpu.make_async_copy(back_a.at[half], atm_out.at[:, :, cut], out_sem.at[half]))
    for c in atm_store:
        c.start()
    near_own(2)
    for n in range(4, 8):
        split_weights(n)
    relay(2)
    sea_piece(1)
    far_own(2)
    near_relayed(2)
    far_relayed(1)
    relay(3)
    sea_depthwise((0, 1, 2), tuple(range(3, 9)))
    sea_depthwise((13, 14, 15), tuple(range(13, 19)))
    near_own(3)
    far_own(3)
    far_relayed(2)

    for n in (0, 1, 4, 5):
        sea_copies[2 + n].wait_recv()
    for c in sea_copies[:2]:
        c.wait_recv()
    for r in range(3):
        turn_sea(sw[r], st, r)
        sea_edges(r, 0, OR - 3 + r)
        turn_sea(sw[3 + OR + r], st, 3 + OR + r)
        sea_edges(3 + OR + r, 2, r)

    @pl.when(tile == 0)
    def _():
        st[0:3] = jnp.zeros((3, COLS + 2 * EDGE, 128), F32)

    @pl.when(top)
    def _():
        for c in fold:
            c.wait()
        flip = 127 - lax.broadcasted_iota(jnp.int32, (CO, 128), 1)
        for k in range(3):
            first = jnp.take_along_axis(mirror_w[2 - k, :, 128:256], flip, axis=1)
            second = jnp.take_along_axis(mirror_w[2 - k, :, 0:128], flip, axis=1)
            turn_sea(jnp.concatenate([first, second], axis=1), st, 19 + k)
            for c in range(3):
                st[19 + k, pl.ds(EDGE - 3 + c, 1), :] = mirror_in[pl.ds(8 * (2 - k) + 4 + 2 - c, 1), :]
                st[19 + k, pl.ds(EDGE + COLS + c, 1), :] = mirror_in[pl.ds(8 * (2 - k) + 2 - c, 1), :]

    sea_depthwise((0, 1, 2), (0, 1, 2), True)
    sea_depthwise((13, 14, 15), (19, 20, 21), True)
    sea_piece(2)
    sea_piece(3)
    near_relayed(3)
    far_relayed(3)
    for stage in range(4):
        finish(stage)

    def flux_of(block):
        live = count[block]
        picked = []
        for k in range(4):
            index = src[k, block]
            t, a = index // 16, lax.rem(index, 16)
            r = a // 2
            spot = jnp.where(r < 4, (3 - r) * 4, (r - 4) * 4 + 2) + lax.rem(a, 2)
            picked.append(jnp.where(k < live, blocks[t, spot], 0.0))
        hi, lo = split(jnp.concatenate(picked, axis=1))
        both = mm(jnp.concatenate([hi, lo], axis=0), w_cat[block])
        flux = both[0:FL, 0:128] + (both[0:FL, 128:256] + both[FL : 2 * FL, 0:128])
        hi = flux.astype(BF16).astype(F32)
        turned = jnp.transpose(jnp.concatenate([hi, flux - hi], axis=0)).astype(BF16)
        return jnp.concatenate([turned, turned], axis=1)

    def sea_rows(q, n):
        flux = jnp.concatenate([flux_of(2 * q + i) for i in range(2 * n)], axis=0)
        grown = gelu(pre[pl.ds(q, n)].reshape(n * COLS, HO) + mm(flux, wic_s[...]))
        out = mm(jnp.concatenate(split(grown), axis=1), wo_s[...])
        out = out[:, 0:128] + out[:, 128:256]
        for i in range(n):
            for half in range(2):
                at_cell = i * COLS + half * 128
                value = jnp.transpose(out[at_cell : at_cell + 128])[0:CO]
                value = value + sw[3 + q + i, :, half * 128 : half * 128 + 128]
                back_s.at[half].reshape(CO * OR, 128)[pl.ds(q + i, CO, stride=OR), :] = value

    sea_store = []
    for part in range(2):

        def step(i, carry, part=part):
            sea_rows(8 * part + 4 * i, 2)
            sea_rows(8 * part + 4 * i + 2, 2)
            return carry

        lax.fori_loop(0, 2, step, 0)
        for half in range(2):
            rows, cut = pl.ds(8 * part, 8), pl.ds(128 * half, 128)
            c = pltpu.make_async_copy(
                back_s.at[half, :, rows], sea_out.at[:, rows, cut], out_sem.at[2 + 2 * part + half]
            )
            c.start()
            sea_store.append(c)
    for c in row_copies + edge_copies + sea_copies + sent:
        c.wait_send()
    for c in atm_store + sea_store:
        c.wait()


def step(src, count, atmosphere, ocean, weights, *params):
    return pl.pallas_call(
        fused_kernel,
        out_shape=(
            jax.ShapeDtypeStruct((CA, AR, COLS), F32),
            jax.ShapeDtypeStruct((CO, OR, COLS), F32),
        ),
        in_specs=[SMEM, SMEM, ANY, ANY, ANY] + [VMEM] * 8,
        out_specs=(ANY, ANY),
        scratch_shapes=[
            pltpu.VMEM((2, CA, AR, 128), F32),
            pltpu.VMEM((2, CO, OR, 128), F32),
            pltpu.VMEM((AR + 6, CA, COLS), F32),
            pltpu.VMEM((AR + 6, COLS + 2 * EDGE, 128), F32),
            pltpu.VMEM((AR + 6, 128 + 2 * EDGE, 128), F32),
            pltpu.VMEM((OR + 6, CO, COLS), F32),
            pltpu.VMEM((OR + 6, COLS + 2 * EDGE, 128), F32),
            pltpu.VMEM((2, 64, 128), F32),
            pltpu.VMEM((2, 3, 64, 128), F32),
            pltpu.VMEM((2, 64, 128), F32),
            pltpu.VMEM((2, 3, 64, 128), F32),
            pltpu.VMEM((3, CO, COLS), F32),
            pltpu.VMEM((24, 128), F32),
            pltpu.VMEM((24, 128), F32),
            pltpu.VMEM((49, 8, 128), F32),
            pltpu.VMEM((49, 8, 128), F32),
            pltpu.VMEM((49, 8, 128), F32),
            pltpu.VMEM((AR, 256, 128), F32),
            pltpu.VMEM((AR, 128, 128), F32),
            pltpu.VMEM((OR, 256, 128), F32),
            pltpu.VMEM((2, 3, 512, 256), BF16),
            pltpu.VMEM((2 * CA, HA), BF16),
            pltpu.VMEM((2 * FL, CA), BF16),
            pltpu.VMEM((2, HA, 2 * COLS), BF16),
            pltpu.VMEM((384, HO), BF16),
            pltpu.VMEM((2 * HO, 256), BF16),
            pltpu.VMEM((4 * FL, HO), BF16),
            pltpu.VMEM((OR, COLS, HO), F32),
            pltpu.VMEM((N_TILE, 16, FL, 128), F32),
            pltpu.VMEM((2, 4, 4, 128, 128), F32),
            pltpu.VMEM((32, 512, 256), BF16),
            pltpu.VMEM((2, CA, AR, 128), F32),
            pltpu.VMEM((2, CO, OR, 128), F32),
            DMA((4,)),
            DMA((2,)),
            DMA((6,)),
            DMA((22,)),
            DMA((22,)),
            DMA((4, 15)),
            DMA((4, 15)),
        ],
        compiler_params=pltpu.CompilerParams(
            collective_id=0, has_side_effects=True, vmem_limit_bytes=57 * MIB
        ),
        name="coupled",
    )(src, count, atmosphere, ocean, weights, *params)


def hand_over_kernel(atm, sea, atm_out, sea_out, atm_here, sea_here, in_sem, out_sem):
    loads, stores = [], []
    for n in range(8):
        size, frm, here, to = ((CA, atm, atm_here, atm_out), (CO, sea, sea_here, sea_out))[n % 2]
        part = pl.ds(n // 2 * (size // 4), size // 4)
        loads.append(pltpu.make_async_copy(frm.at[part], here.at[part], in_sem.at[n]))
        stores.append(pltpu.make_async_copy(here.at[part], to.at[part], out_sem.at[n]))
    for c in loads:
        c.start()
    for load, store in zip(loads, stores):
        load.wait()
        store.start()
    for c in stores:
        c.wait()


def hand_over(atm, sea):
    shapes = ((CA, AR, COLS), (CO, OR, COLS))
    return pl.pallas_call(
        hand_over_kernel,
        out_shape=tuple(jax.ShapeDtypeStruct(shape, F32) for shape in shapes),
        in_specs=[ANY, ANY],
        out_specs=(ANY, ANY),
        scratch_shapes=[*(pltpu.VMEM(shape, F32) for shape in shapes), DMA((8,)), DMA((8,))],
        compiler_params=pltpu.CompilerParams(vmem_limit_bytes=58 * MIB),
        name="hand_over",
    )(atm, sea)


def body(
    atmosphere, ocean, kernel_atm, w_in_atm, w_out_atm, w_flux, kernel_ocean, w_in_ocean,
    w_out_ocean, w_couple, intersection_src, intersection_count, intersection_weight,
):
    results = step(
        intersection_src[0].T, intersection_count[0], atmosphere, ocean, intersection_weight[0],
        kernel_atm.T, w_in_atm, w_out_atm, w_flux, kernel_ocean.T, w_in_ocean, w_out_ocean, w_couple.T,
    )
    return hand_over(*results)


def solution(mesh):
    return jax.shard_map(
        body,
        mesh=mesh,
        in_specs=(
            P(None, "face", "tile"),
            P(None, "tile", "face"),
            P(), P(), P(), P(), P(), P(), P(), P(),
            P("face", "tile", None),
            P("face", "tile"),
            P("face", "tile", None, None, None),
        ),
        out_specs=(P(None, "face", "tile"), P(None, "tile", "face")),
        check_vma=False,
    )
```
